32 devices in a mesh: dp: 4 (over z), seq: 8 (over y, x, core).
Axes of the slice: x: 2, y: 2, z: 4, core: 2. Of those that a mesh axis runs over, the one named last changes fastest.
Arguments:
- tokens: bfloat16 [4096, 8192], P(('dp', 'seq')), may hold values from -6 to 6
- queries: bfloat16 [4096, 1024], P(('dp', 'seq')), may hold values from -110 to 110
- positions: int32 [4096], P(('dp', 'seq')), may hold values from 0 to 255, as said below
- grad: float32 [8192, 256], P(('dp', 'seq')), may hold values from -6 to 6
- master: float32 [8192, 256], P(('dp', 'seq')), may hold values from -0.0625 to 0.0625
- moment1: float32 [8192, 256], P(('dp', 'seq')), may hold values from -1.8 to 1.8
- moment2: float32 [8192, 256], P(('dp', 'seq')), may hold values from 0.5 to 4
- step: int32 [1], replicated, may hold values from 1 to 8
Outputs:
- attention: bfloat16 [4096, 1024], P(('dp', 'seq'))
- new_master: float32 [8192, 256], P(('dp', 'seq'))
- new_first: float32 [8192, 256], P(('dp', 'seq'))
- new_second: float32 [8192, 256], P(('dp', 'seq'))
The draws below stay inside these ranges and needn't reach their ends.
Inputs may be any that keep to these rules, and one draw needn't show every extreme that they name: `positions`: the sequence is a pack of documents of 1 to 256 tokens, one of exactly 256; a position is 0 at the first token of each document and rises by one from token to token inside a document.
All inputs are finite; a program needn't handle non-finite values.
Results may differ from the reference program's by a relative error of at most 0.014.
The reference program's roundings to bfloat16 on the way (of `weight`, `rotated` and `probs`) count: a program that leaves them out, or rounds other values in their place, can miss the bound.
Values may be sent and summed in bfloat16 or wider, within the bound.
A program may use at most 64 MiB of HBM per device.

```python
import math
import jax
import jax.numpy as jnp
from jax import lax

D = 8192
HD = 128
GROUP = 8
TOK_DEV = 128
DOC_MAX = 256
SEQLEN = 4096


def draw_queries(key, part):
    shape = (SEQLEN, GROUP * HD)
    key_base = jax.random.fold_in(key, 11)
    values_out = jnp.clip(jax.random.normal(key_base, shape, jnp.float32), -6.0, 6.0)
    return values_out.astype(jnp.bfloat16)


def draw_positions(key, part):
    length_key = jax.random.fold_in(key, 21)
    index = jnp.arange(SEQLEN, dtype=jnp.int32)
    lengths = jax.random.randint(length_key, (SEQLEN,), 1, DOC_MAX + 1).astype(jnp.int32)
    lengths = jnp.where(index == 0, DOC_MAX, lengths).astype(jnp.int32)
    ends = jnp.cumsum(lengths).astype(jnp.int32)
    starts = (ends - lengths).astype(jnp.int32)
    doc_ids = jnp.searchsorted(ends, index, side='right').astype(jnp.int32)
    return (index - starts[doc_ids]).astype(jnp.int32)


def steps_of(own_key, dims, cuts, smallest, largest):
    factor_of, own = 1.0, jax.random.fold_in(own_key, 6)
    for position, blocks in cuts:
        heights = jnp.exp(jax.random.uniform(jax.random.fold_in(own, position), (blocks,), jnp.float32, smallest / len(cuts), largest / len(cuts)))
        factor_of = factor_of * jnp.repeat(heights, dims[position] // blocks).reshape([-1 if axis == position else 1 for axis in range(len(dims))])
    return factor_of


def noise(rng, extent, width, reach, pieces=(), kind=jnp.bfloat16):
    result = jax.random.normal(rng, extent, jnp.float32) * width
    if len(pieces) > 0:
        result = steps_of(rng, extent, pieces, -0.22, 0.18) * result
    return jnp.clip(result, min=-reach, max=reach).astype(kind)


def setup_inputs(seed: int = 0) -> dict:
    arg_keys = jax.random.split(jax.random.key(seed), 9)
    return {
        "tokens": noise(arg_keys[0], (SEQLEN, D), 1.0, 6.0, ((0, 32),)),
        "queries": draw_queries(jax.random.fold_in(arg_keys[8], 71), 0),
        "positions": draw_positions(jax.random.fold_in(arg_keys[8], 71), 0),
        "grad": noise(arg_keys[3], (D, 2 * HD), 1.0, 6.0, ((0, 32),), jnp.float32),
        "master": noise(arg_keys[4], (D, 2 * HD), D ** -0.5, 0.0625, ((0, 32),), jnp.float32),
        "moment1": noise(arg_keys[5], (D, 2 * HD), 0.3, 1.8, ((0, 32),), jnp.float32),
        "moment2": jnp.clip(jnp.exp(math.log(4.0) - 2.0794415 * jax.random.uniform(arg_keys[6], (D, 2 * HD), jnp.float32) ** steps_of(arg_keys[6], (D, 2 * HD), ((0, 32),), -0.2, 0.2)), 0.5, 4.0),
        "step": jax.random.randint(arg_keys[7], (1,), 1, 9).astype(jnp.int32),
    }


beta_one = 0.9
beta_two = 0.95
learn_rate = 0.02
adam_eps = 1e-08
rope_base = 500000.0
masked_score = -1e+30

def rotate_pairs(values_in, places):
    half_width = values_in.shape[-1] // 2
    freqs = jnp.exp(jnp.arange(half_width, dtype=jnp.float32) * (-2.0 * math.log(rope_base) / values_in.shape[-1]))
    angles = places.astype(jnp.float32)[:, None, None] * freqs
    cosine = jnp.cos(angles)
    sine = jnp.sin(angles)
    first = values_in[..., :half_width]
    second = values_in[..., half_width:]
    return jnp.concatenate([first * cosine - second * sine, second * cosine + first * sine], axis=-1)

def adam_update(grad, master, moment1, moment2, step):
    counter = step[0].astype(jnp.float32)
    new_first = beta_one * moment1 + (1.0 - beta_one) * grad
    new_second = beta_two * moment2 + (1.0 - beta_two) * grad * grad
    fixed_first = new_first / (1.0 - jnp.power(jnp.float32(beta_one), counter))
    fixed_second = new_second / (1.0 - jnp.power(jnp.float32(beta_two), counter))
    new_master = master - learn_rate * fixed_first / (jnp.sqrt(fixed_second) + adam_eps)
    return (new_master, new_first, new_second)

def attend_rows(query_rows, query_global, query_places, keys, values_v, key_global):
    row_count = query_rows.shape[0]
    block = 512 if row_count % 512 == 0 else row_count

    def one_block(triple):
        rows, index, places = triple
        scores = jnp.dot(rows, keys.T, preferred_element_type=jnp.float32) * rows.shape[-1] ** (-0.5)
        allowed = (key_global[None, :] <= index[:, None]) & (key_global[None, :] >= (index - places)[:, None])
        scores = jnp.where(allowed, scores, masked_score)
        top_score = lax.optimization_barrier(jnp.max(scores, axis=1, keepdims=True))
        weights = jnp.exp(scores - top_score)
        totals = lax.optimization_barrier(jnp.sum(weights, axis=1, keepdims=True))
        probs = (weights / totals).astype(jnp.bfloat16)
        return jnp.dot(probs, values_v, preferred_element_type=jnp.float32).astype(jnp.bfloat16)
    blocks = lax.map(one_block, (query_rows.reshape(-1, block, query_rows.shape[1]), query_global.reshape(-1, block), query_places.reshape(-1, block)))
    return blocks.reshape(row_count, -1)

def reference(tokens, queries, positions, grad, master, moment1, moment2, step):
    new_master, new_first, new_second = adam_update(grad, master, moment1, moment2, step)
    weight = new_master.astype(jnp.bfloat16)
    head_dim = weight.shape[1] // 2
    projected = jnp.dot(tokens, weight, preferred_element_type=jnp.float32)
    keys = rotate_pairs(projected[:, None, :head_dim], positions)[:, 0].astype(jnp.bfloat16)
    values_v = projected[:, head_dim:].astype(jnp.bfloat16)
    rotated = rotate_pairs(queries.astype(jnp.float32).reshape(SEQLEN, GROUP, head_dim), positions).astype(jnp.bfloat16)
    padded_keys = jnp.concatenate([jnp.zeros((DOC_MAX, head_dim), keys.dtype), keys], axis=0)
    padded_values = jnp.concatenate([jnp.zeros((DOC_MAX, head_dim), values_v.dtype), values_v], axis=0)
    local_index = jnp.arange(TOK_DEV, dtype=jnp.int32)
    window_index = jnp.arange(DOC_MAX + TOK_DEV, dtype=jnp.int32)

    def one_block(start):
        rows = lax.dynamic_slice_in_dim(rotated, start, TOK_DEV, 0).reshape(TOK_DEV * GROUP, head_dim)
        places = lax.dynamic_slice_in_dim(positions, start, TOK_DEV, 0)
        query_global = jnp.repeat(start + local_index, GROUP)
        query_places = jnp.repeat(places, GROUP)
        block_keys = lax.dynamic_slice_in_dim(padded_keys, start, DOC_MAX + TOK_DEV, 0)
        block_values = lax.dynamic_slice_in_dim(padded_values, start, DOC_MAX + TOK_DEV, 0)
        key_global = start - DOC_MAX + window_index
        return attend_rows(rows, query_global, query_places, block_keys, block_values, key_global).reshape(TOK_DEV, GROUP * head_dim)
    starts = jnp.arange(SEQLEN // TOK_DEV, dtype=jnp.int32) * TOK_DEV
    attention = lax.map(one_block, starts).reshape(SEQLEN, GROUP * head_dim)
    return (attention, new_master, new_first, new_second)
```

```python
import math

import jax
import jax.numpy as jnp
from jax import lax
from jax.experimental import pallas as pl
from jax.experimental.pallas import tpu as pltpu
from jax.sharding import PartitionSpec as P

GROUP = 8
MESH = pl.DeviceIdType.MESH


beta_one = 0.9
beta_two = 0.95
learn_rate = 0.02
adam_eps = 1e-08
rope_base = 500000.0
masked_score = -1e30


def shifted(value, axis, steps):
    count = lax.axis_size(axis)
    first, last = (max(0, -steps), min(count, count - steps))
    return lax.ppermute(value, axis, [(source, source + steps) for source in range(first, last)])


def rotate_pairs(values_in, places):
    half_width = values_in.shape[-1] // 2
    freqs = jnp.exp(
        jnp.arange(half_width, dtype=jnp.float32)
        * (-2.0 * math.log(rope_base) / values_in.shape[-1])
    )
    angles = places.astype(jnp.float32)[:, None, None] * freqs
    cosine = jnp.cos(angles)
    sine = jnp.sin(angles)
    first = values_in[..., :half_width]
    second = values_in[..., half_width:]
    return jnp.concatenate(
        [first * cosine - second * sine, second * cosine + first * sine], axis=-1
    )


def adam_update(grad, master, moment1, moment2, step):
    counter = step[0].astype(jnp.float32)
    new_first = beta_one * moment1 + (1.0 - beta_one) * grad
    new_second = beta_two * moment2 + (1.0 - beta_two) * grad * grad
    fixed_first = new_first / (1.0 - jnp.power(jnp.float32(beta_one), counter))
    fixed_second = new_second / (1.0 - jnp.power(jnp.float32(beta_two), counter))
    new_master = master - learn_rate * fixed_first / (jnp.sqrt(fixed_second) + adam_eps)
    return (new_master, new_first, new_second)


def attend_rows(query_rows, query_global, query_places, keys, values_v, key_global):
    row_count = query_rows.shape[0]
    block = 512

    def one_block(triple):
        rows, index, places = triple
        scores = jnp.einsum(
            "rd,kd->rk", rows, keys, preferred_element_type=jnp.float32
        ) * rows.shape[-1] ** (-0.5)
        allowed = (key_global[None, :] <= index[:, None]) & (
            key_global[None, :] >= (index - places)[:, None]
        )
        scores = jnp.where(allowed, scores, masked_score)
        top_score = jnp.max(scores, axis=1, keepdims=True)
        weights = jnp.exp(scores - top_score)
        totals = jnp.sum(weights, axis=1, keepdims=True)
        probs = (weights / totals).astype(jnp.bfloat16)
        return jnp.dot(probs, values_v, preferred_element_type=jnp.float32).astype(jnp.bfloat16)

    blocks = lax.map(
        one_block,
        (
            query_rows.reshape(-1, block, query_rows.shape[1]),
            query_global.reshape(-1, block),
            query_places.reshape(-1, block),
        ),
    )
    return blocks.reshape(row_count, -1)


def local(tokens, queries, positions, grad, master, moment1, moment2, step):
    new_master, new_first, new_second = adam_update(grad, master, moment1, moment2, step)
    weight = new_master.astype(jnp.bfloat16)
    head_dim = weight.shape[1] // 2
    local_count = tokens.shape[0]
    projected = jnp.dot(
        tokens,
        lax.all_gather(weight, ("dp", "seq"), axis=0, tiled=True),
        preferred_element_type=jnp.float32,
    )
    local_keys = rotate_pairs(projected[:, None, :head_dim], positions)[:, 0]
    key_value = jnp.concatenate([local_keys, projected[:, head_dim:]], axis=1).astype(jnp.bfloat16)
    group_kv = lax.all_gather(key_value, "seq", axis=0, tiled=True)
    span = group_kv.shape[0]
    reach = span // 4
    earlier = shifted(group_kv[span - reach :], "dp", 1)
    window = jnp.concatenate([earlier, group_kv], axis=0)
    group_index = lax.axis_index("dp")
    my_index = lax.axis_index("seq")
    window_start = group_index * span - reach
    rotated = rotate_pairs(
        queries.astype(jnp.float32).reshape(local_count, GROUP, head_dim), positions
    ).astype(jnp.bfloat16)
    offset = my_index * local_count
    near = lax.dynamic_slice_in_dim(window, offset, reach + local_count, 0)
    key_global = window_start + offset + jnp.arange(reach + local_count, dtype=jnp.int32)
    query_global = jnp.repeat(
        group_index * span + offset + jnp.arange(local_count, dtype=jnp.int32), GROUP
    )
    query_places = jnp.repeat(positions, GROUP)
    results = attend_rows(
        rotated.reshape(local_count * GROUP, head_dim),
        query_global,
        query_places,
        near[:, :head_dim],
        near[:, head_dim:],
        key_global,
    )
    attention = results.reshape(local_count, GROUP * head_dim)
    return (attention, new_master, new_first, new_second)


def rope_tables(places, width):
    lane = lax.broadcasted_iota(jnp.int32, (1, width), 1)
    half_width = width // 2
    slot = jnp.where(lane < half_width, lane, lane - half_width).astype(jnp.float32)
    freqs = jnp.exp(slot * (-2.0 * math.log(rope_base) / width))
    angles = places.astype(jnp.float32) * freqs
    sine = jnp.sin(angles)
    return jnp.cos(angles), jnp.where(lane < half_width, -sine, sine)


def fused_kernel(
    tok_hbm, query_hbm, weight_ref, places_ref, out_ref,
    tok, blocks, query, rotated, part, back, kv, cosine, sine,
    tok_sem, tok_send, tok_recv, query_sem, block_recv, half_recv,
    x_send, y_send, z_send, cross_send, half_x_send, half_y_send,
    back_sems, kv_send, kv_recv,
):
    z = lax.axis_index("dp")
    seq = lax.axis_index("seq")
    planes = lax.axis_size("dp")
    wide = lax.axis_size("seq")
    core = lax.rem(seq, 2)
    x = lax.rem(seq // 2, 2)
    y = seq // 4
    count = tok_hbm.shape[0]
    depth = weight_ref.shape[0]
    half = depth // 2
    head_dim = weight_ref.shape[1] // 2
    me = z * wide + seq
    total = planes * wide
    chips = blocks.shape[0]

    def ordinal(index):
        return (index // wide, lax.rem(index, wide))

    peer = (z, seq + 1 - 2 * core)
    x_side = (z, seq + 2 - 4 * x)
    y_side = (z, seq + 4 - 8 * y)
    z_pair = z + 1 - 2 * lax.rem(z, 2)
    pair_side = (z_pair, seq)
    cross_side = (3 - z, seq)
    inner = (z == 1) | (z == 2)
    next_one, next_two = lax.rem(me + 1, total), lax.rem(me + 2, total)
    last_one, last_two = lax.rem(me + total - 1, total), lax.rem(me + total - 2, total)

    barrier = pltpu.get_barrier_semaphore()
    greeted = [peer, x_side, y_side, pair_side, cross_side]
    greeted += [ordinal(index) for index in (next_one, next_two, last_one, last_two)]
    for device in greeted:
        pl.semaphore_signal(barrier, inc=1, device_id=device, device_id_type=MESH)

    def columns(chip, which):
        return pl.ds(pl.multiple_of((chip * 2 + which) * depth, depth), depth)

    def rows_of(which):
        return pl.ds(pl.multiple_of(which * count, count), count)

    def local_tokens(chip):
        return pltpu.make_async_copy(
            tok_hbm.at[:, columns(chip, core)], tok.at[chip, rows_of(core)], tok_sem.at[chip]
        )

    def sent_tokens(chip):
        return pltpu.make_async_remote_copy(
            src_ref=tok_hbm.at[:, columns(chip, 1 - core)],
            dst_ref=tok.at[chip, rows_of(core)],
            send_sem=tok_send.at[chip],
            recv_sem=tok_recv.at[chip],
            device_id=peer,
            device_id_type=MESH,
        )

    query_copy = pltpu.make_async_copy(query_hbm, query, query_sem)
    pl.semaphore_wait(barrier, len(greeted))

    order = [z, z_pair, 2 - z // 2, 3 - 3 * (z // 2)]

    def chip_at(plane, y_at, x_at):
        return plane * 4 + y_at * 2 + x_at

    def send_block(step, device, sem):
        chip = chip_at(order[step], y, x)
        return pltpu.make_async_remote_copy(
            src_ref=weight_ref if step == 0 else blocks.at[chip],
            dst_ref=blocks.at[chip],
            send_sem=sem.at[step],
            recv_sem=block_recv.at[chip],
            device_id=device,
            device_id_type=MESH,
        )

    def send_half(step, which):
        chip = chip_at(order[step], y, 1 - x) if which == 0 else chip_at(order[step], 1 - y, x)
        return pltpu.make_async_remote_copy(
            src_ref=blocks.at[chip, pl.ds(which * half, half)],
            dst_ref=blocks.at[chip, pl.ds(which * half, half)],
            send_sem=(half_y_send if which == 0 else half_x_send).at[step],
            recv_sem=half_recv.at[which, chip],
            device_id=y_side if which == 0 else x_side,
            device_id_type=MESH,
        )

    def block_arrival(chip):
        pltpu.make_async_copy(blocks.at[chip], blocks.at[chip], block_recv.at[chip]).wait()

    def half_arrival(which, chip):
        place = blocks.at[chip, pl.ds(which * half, half)]
        pltpu.make_async_copy(place, place, half_recv.at[which, chip]).wait()

    def add_block(chip, source):
        local_tokens(chip).wait()
        sent_tokens(chip).wait_recv()
        part[...] += jnp.dot(tok[chip], source[...], preferred_element_type=jnp.float32)

    steps = len(order)
    for device, sem in ((x_side, x_send), (y_side, y_send), (pair_side, z_send)):
        send_block(0, device, sem).start()

    @pl.when(inner)
    def _():
        send_block(0, cross_side, cross_send).start()

    query_copy.start()

    @pl.loop(0, chips)
    def _(chip):
        sent_tokens(chip).start()
        local_tokens(chip).start()

    part[...] = jnp.zeros_like(part)

    row = lax.broadcasted_iota(jnp.int32, (count, count), 0)
    lane = lax.broadcasted_iota(jnp.int32, (count, count), 1)
    places = jnp.sum(
        jnp.where(row == lane, places_ref[...].astype(jnp.float32), 0.0), axis=1, keepdims=True
    )
    cosine[...], sine[...] = rope_tables(places, head_dim)

    def rotate(values_in):
        return values_in * cosine[...] + pltpu.roll(values_in, head_dim // 2, 1) * sine[...]

    query_copy.wait()
    heads = query.shape[1] // head_dim
    for head in range(heads):
        at = slice(head * head_dim, (head + 1) * head_dim)
        rotated[:, at] = rotate(query[:, at].astype(jnp.float32)).astype(jnp.bfloat16)
    add_block(chip_at(z, y, x), weight_ref)

    for step in range(1, steps + 1):
        if step < steps:
            chip = chip_at(order[step], y, x)
            block_arrival(chip)

            @pl.when(inner)
            def _():
                if step == 1:
                    send_block(step, cross_side, cross_send).start()
                else:
                    send_block(step, pair_side, z_send).start()

            send_block(step, x_side, x_send).start()
            send_block(step, y_side, y_send).start()
            add_block(chip, blocks.at[chip])
        across = [chip_at(order[step - 1], y, 1 - x), chip_at(order[step - 1], 1 - y, x)]
        for which in range(2):
            block_arrival(across[which])
            send_half(step - 1, which).start()
        for chip in across:
            add_block(chip, blocks.at[chip])
        if step > 1:
            chip = chip_at(order[step - 2], 1 - y, 1 - x)
            half_arrival(0, chip)
            half_arrival(1, chip)
            add_block(chip, blocks.at[chip])
    chip = chip_at(order[steps - 1], 1 - y, 1 - x)
    half_arrival(0, chip)
    half_arrival(1, chip)
    add_block(chip, blocks.at[chip])

    back_copy = pltpu.make_async_remote_copy(
        src_ref=part.at[rows_of(1 - core)],
        dst_ref=back,
        send_sem=back_sems.at[0],
        recv_sem=back_sems.at[1],
        device_id=peer,
        device_id_type=MESH,
    )
    back_copy.start()
    back_copy.wait_recv()
    projected = part[rows_of(core)] + back[...]
    own = pl.ds(2 * count, count)
    kv[own, :head_dim] = rotate(projected[:, :head_dim]).astype(jnp.bfloat16)
    kv[own, head_dim:] = projected[:, head_dim:].astype(jnp.bfloat16)

    def send_kv(distance):
        return pltpu.make_async_remote_copy(
            src_ref=kv.at[own],
            dst_ref=kv.at[pl.ds((2 - distance) * count, count)],
            send_sem=kv_send.at[distance - 1],
            recv_sem=kv_recv.at[distance - 1],
            device_id=ordinal(next_one if distance == 1 else next_two),
            device_id_type=MESH,
        )

    for distance in (1, 2):

        @pl.when(me < total - distance)
        def _():
            send_kv(distance).start()

        @pl.when(me < distance)
        def _():
            kv[pl.ds((2 - distance) * count, count), :] = jnp.zeros(
                (count, 2 * head_dim), jnp.bfloat16
            )

    key_row = lax.broadcasted_iota(jnp.int32, (count, 3 * count), 1) - 2 * count
    query_row = lax.broadcasted_iota(jnp.int32, (count, 3 * count), 0)
    allowed = (key_row <= query_row) & (key_row >= query_row - places.astype(jnp.int32))

    for distance in (1, 2):

        @pl.when(me >= distance)
        def _():
            send_kv(distance).wait_recv()

    keys = kv[:, :head_dim]
    values_v = kv[:, head_dim:]
    for head in range(heads):
        at = slice(head * head_dim, (head + 1) * head_dim)
        scores = lax.dot_general(
            rotated[:, at], keys, (((1,), (1,)), ((), ())), preferred_element_type=jnp.float32
        ) * head_dim ** (-0.5)
        scores = jnp.where(allowed, scores, masked_score)
        weights = jnp.exp(scores - jnp.max(scores, axis=1, keepdims=True))
        probs = (weights * (1.0 / jnp.sum(weights, axis=1, keepdims=True))).astype(jnp.bfloat16)
        out_ref[:, at] = jnp.dot(probs, values_v, preferred_element_type=jnp.float32).astype(
            jnp.bfloat16
        )

    for step in range(steps):
        send_block(step, x_side, x_send).wait_send()
        send_block(step, y_side, y_send).wait_send()
        send_half(step, 0).wait_send()
        send_half(step, 1).wait_send()
    send_block(0, pair_side, z_send).wait_send()

    @pl.when(inner)
    def _():
        send_block(2, pair_side, z_send).wait_send()
        send_block(3, pair_side, z_send).wait_send()
        send_block(0, cross_side, cross_send).wait_send()
        send_block(1, cross_side, cross_send).wait_send()

    @pl.loop(0, chips)
    def _(chip):
        sent_tokens(chip).wait_send()

    back_copy.wait_send()
    for distance in (1, 2):

        @pl.when(me < total - distance)
        def _():
            send_kv(distance).wait_send()


def fused_local(tokens, queries, positions, grad, master, moment1, moment2, step):
    new_master, new_first, new_second = adam_update(grad, master, moment1, moment2, step)
    weight = new_master.astype(jnp.bfloat16)
    count = tokens.shape[0]
    depth, width = weight.shape
    head_dim = width // 2
    chips = tokens.shape[1] // depth // 2
    dma = pltpu.SemaphoreType.DMA
    anywhere = pl.BlockSpec(memory_space=pl.ANY)
    inside = pl.BlockSpec(memory_space=pltpu.VMEM)
    attention = pl.pallas_call(
        fused_kernel,
        out_shape=jax.ShapeDtypeStruct(queries.shape, jnp.bfloat16),
        in_specs=[anywhere, anywhere, inside, inside],
        out_specs=inside,
        scratch_shapes=[
            pltpu.VMEM((chips, 2 * count, depth), jnp.bfloat16),
            pltpu.VMEM((chips, depth, width), jnp.bfloat16),
            pltpu.VMEM(queries.shape, jnp.bfloat16),
            pltpu.VMEM(queries.shape, jnp.bfloat16),
            pltpu.VMEM((2 * count, width), jnp.float32),
            pltpu.VMEM((count, width), jnp.float32),
            pltpu.VMEM((3 * count, width), jnp.bfloat16),
            pltpu.VMEM((count, head_dim), jnp.float32),
            pltpu.VMEM((count, head_dim), jnp.float32),
            dma((chips,)), dma((chips,)), dma((chips,)), dma,
            dma((chips,)), dma((2, chips)),
            dma((4,)), dma((4,)), dma((4,)), dma((4,)), dma((4,)), dma((4,)),
            dma((2,)), dma((2,)), dma((2,)),
        ],
        compiler_params=pltpu.CompilerParams(
            collective_id=0, has_side_effects=True, vmem_limit_bytes=40 * 1024 * 1024
        ),
    )(tokens, queries, weight, positions.reshape(1, -1))
    return (attention, new_master, new_first, new_second)


def solution(mesh):
    small = (mesh.shape["dp"], mesh.shape["seq"]) == (4, 8)
    return jax.shard_map(
        fused_local if small else local,
        mesh=mesh,
        in_specs=(
            P(("dp", "seq"), None),
            P(("dp", "seq"), None),
            P(("dp", "seq")),
            P(("dp", "seq"), None),
            P(("dp", "seq"), None),
            P(("dp", "seq"), None),
            P(("dp", "seq"), None),
            P(),
        ),
        out_specs=(
            P(("dp", "seq"), None),
            P(("dp", "seq"), None),
            P(("dp", "seq"), None),
            P(("dp", "seq"), None),
        ),
        check_vma=False,
    )
```

```python
import math

import jax
import jax.numpy as jnp
from jax import lax
from jax.experimental import pallas as pl
from jax.experimental.pallas import tpu as pltpu
from jax.sharding import PartitionSpec as P

GROUP = 8
MESH = pl.DeviceIdType.MESH


beta_one = 0.9
beta_two = 0.95
learn_rate = 0.02
adam_eps = 1e-08
rope_base = 500000.0
masked_score = -1e30


def shifted(value, axis, steps):
    count = lax.axis_size(axis)
    first, last = (max(0, -steps), min(count, count - steps))
    return lax.ppermute(value, axis, [(source, source + steps) for source in range(first, last)])


def rotate_pairs(values_in, places):
    half_width = values_in.shape[-1] // 2
    freqs = jnp.exp(
        jnp.arange(half_width, dtype=jnp.float32)
        * (-2.0 * math.log(rope_base) / values_in.shape[-1])
    )
    angles = places.astype(jnp.float32)[:, None, None] * freqs
    cosine = jnp.cos(angles)
    sine = jnp.sin(angles)
    first = values_in[..., :half_width]
    second = values_in[..., half_width:]
    return jnp.concatenate(
        [first * cosine - second * sine, second * cosine + first * sine], axis=-1
    )


def adam_update(grad, master, moment1, moment2, step):
    counter = step[0].astype(jnp.float32)
    new_first = beta_one * moment1 + (1.0 - beta_one) * grad
    new_second = beta_two * moment2 + (1.0 - beta_two) * grad * grad
    fixed_first = new_first / (1.0 - jnp.power(jnp.float32(beta_one), counter))
    fixed_second = new_second / (1.0 - jnp.power(jnp.float32(beta_two), counter))
    new_master = master - learn_rate * fixed_first / (jnp.sqrt(fixed_second) + adam_eps)
    return (new_master, new_first, new_second)


def attend_rows(query_rows, query_global, query_places, keys, values_v, key_global):
    row_count = query_rows.shape[0]
    block = 512

    def one_block(triple):
        rows, index, places = triple
        scores = jnp.einsum(
            "rd,kd->rk", rows, keys, preferred_element_type=jnp.float32
        ) * rows.shape[-1] ** (-0.5)
        allowed = (key_global[None, :] <= index[:, None]) & (
            key_global[None, :] >= (index - places)[:, None]
        )
        scores = jnp.where(allowed, scores, masked_score)
        top_score = jnp.max(scores, axis=1, keepdims=True)
        weights = jnp.exp(scores - top_score)
        totals = jnp.sum(weights, axis=1, keepdims=True)
        probs = (weights / totals).astype(jnp.bfloat16)
        return jnp.dot(probs, values_v, preferred_element_type=jnp.float32).astype(jnp.bfloat16)

    blocks = lax.map(
        one_block,
        (
            query_rows.reshape(-1, block, query_rows.shape[1]),
            query_global.reshape(-1, block),
            query_places.reshape(-1, block),
        ),
    )
    return blocks.reshape(row_count, -1)


def local(tokens, queries, positions, grad, master, moment1, moment2, step):
    new_master, new_first, new_second = adam_update(grad, master, moment1, moment2, step)
    weight = new_master.astype(jnp.bfloat16)
    head_dim = weight.shape[1] // 2
    local_count = tokens.shape[0]
    projected = jnp.dot(
        tokens,
        lax.all_gather(weight, ("dp", "seq"), axis=0, tiled=True),
        preferred_element_type=jnp.float32,
    )
    local_keys = rotate_pairs(projected[:, None, :head_dim], positions)[:, 0]
    key_value = jnp.concatenate([local_keys, projected[:, head_dim:]], axis=1).astype(jnp.bfloat16)
    group_kv = lax.all_gather(key_value, "seq", axis=0, tiled=True)
    span = group_kv.shape[0]
    reach = span // 4
    earlier = shifted(group_kv[span - reach :], "dp", 1)
    window = jnp.concatenate([earlier, group_kv], axis=0)
    group_index = lax.axis_index("dp")
    my_index = lax.axis_index("seq")
    window_start = group_index * span - reach
    rotated = rotate_pairs(
        queries.astype(jnp.float32).reshape(local_count, GROUP, head_dim), positions
    ).astype(jnp.bfloat16)
    offset = my_index * local_count
    near = lax.dynamic_slice_in_dim(window, offset, reach + local_count, 0)
    key_global = window_start + offset + jnp.arange(reach + local_count, dtype=jnp.int32)
    query_global = jnp.repeat(
        group_index * span + offset + jnp.arange(local_count, dtype=jnp.int32), GROUP
    )
    query_places = jnp.repeat(positions, GROUP)
    results = attend_rows(
        rotated.reshape(local_count * GROUP, head_dim),
        query_global,
        query_places,
        near[:, :head_dim],
        near[:, head_dim:],
        key_global,
    )
    attention = results.reshape(local_count, GROUP * head_dim)
    return (attention, new_master, new_first, new_second)


def rope_tables(places, width):
    lane = lax.broadcasted_iota(jnp.int32, (1, width), 1)
    half_width = width // 2
    slot = jnp.where(lane < half_width, lane, lane - half_width).astype(jnp.float32)
    freqs = jnp.exp(slot * (-2.0 * math.log(rope_base) / width))
    angles = places.astype(jnp.float32) * freqs
    sine = jnp.sin(angles)
    return jnp.cos(angles), jnp.where(lane < half_width, -sine, sine)


def fused_kernel(
    tok_hbm, query_hbm, weight_ref, places_hbm, out_ref,
    places_ref, own_scores, tok, blocks, query, rotated, part, back, kv, cosine, sine,
    tok_sem, tok_send, tok_recv, query_sem, places_sem, block_recv, half_recv,
    x_send, y_send, z_send, cross_send, half_x_send, half_y_send, across_send,
    back_sems, kv_send, kv_recv,
):
    z = lax.axis_index("dp")
    seq = lax.axis_index("seq")
    planes = lax.axis_size("dp")
    wide = lax.axis_size("seq")
    core = lax.rem(seq, 2)
    x = lax.rem(seq // 2, 2)
    y = seq // 4
    count = tok_hbm.shape[0]
    depth = weight_ref.shape[0]
    half = depth // 2
    head_dim = weight_ref.shape[1] // 2
    me = z * wide + seq
    total = planes * wide
    chips = blocks.shape[0]

    def ordinal(index):
        return (index // wide, lax.rem(index, wide))

    peer = (z, seq + 1 - 2 * core)
    x_side = (z, seq + 2 - 4 * x)
    y_side = (z, seq + 4 - 8 * y)
    z_pair = z + 1 - 2 * lax.rem(z, 2)
    pair_side = (z_pair, seq)
    cross_side = (3 - z, seq)
    inner = (z == 1) | (z == 2)
    next_one, next_two = lax.rem(me + 1, total), lax.rem(me + 2, total)
    last_one, last_two = lax.rem(me + total - 1, total), lax.rem(me + total - 2, total)

    barrier = pltpu.get_barrier_semaphore()
    greeted = [peer, x_side, y_side, pair_side, cross_side]
    greeted += [ordinal(index) for index in (next_one, next_two, last_one, last_two)]
    for device in greeted:
        pl.semaphore_signal(barrier, inc=1, device_id=device, device_id_type=MESH)

    def columns(chip, which):
        return pl.ds(pl.multiple_of((chip * 2 + which) * depth, depth), depth)

    def rows_of(which):
        return pl.ds(pl.multiple_of(which * count, count), count)

    def local_tokens(chip):
        return pltpu.make_async_copy(
            tok_hbm.at[:, columns(chip, core)], tok.at[chip, rows_of(core)], tok_sem.at[chip]
        )

    def sent_tokens(chip):
        return pltpu.make_async_remote_copy(
            src_ref=tok_hbm.at[:, columns(chip, 1 - core)],
            dst_ref=tok.at[chip, rows_of(core)],
            send_sem=tok_send.at[chip],
            recv_sem=tok_recv.at[chip],
            device_id=peer,
            device_id_type=MESH,
        )

    query_copy = pltpu.make_async_copy(query_hbm, query, query_sem)
    places_copy = pltpu.make_async_copy(places_hbm, places_ref, places_sem)
    query_copy.start()
    places_copy.start()
    pl.semaphore_wait(barrier, len(greeted))

    order = [z, z_pair, 2 - z // 2, 3 - 3 * (z // 2)]

    def chip_at(plane, y_at, x_at):
        return plane * 4 + y_at * 2 + x_at

    def send_block(step, device, sem):
        chip = chip_at(order[step], y, x)
        return pltpu.make_async_remote_copy(
            src_ref=weight_ref if step == 0 else blocks.at[chip],
            dst_ref=blocks.at[chip],
            send_sem=sem.at[step],
            recv_sem=block_recv.at[chip],
            device_id=device,
            device_id_type=MESH,
        )

    def send_half(step, which):
        chip = chip_at(order[step], y, 1 - x) if which == 0 else chip_at(order[step], 1 - y, x)
        return pltpu.make_async_remote_copy(
            src_ref=blocks.at[chip, pl.ds(which * half, half)],
            dst_ref=blocks.at[chip, pl.ds(which * half, half)],
            send_sem=(half_y_send if which == 0 else half_x_send).at[step],
            recv_sem=half_recv.at[which, chip],
            device_id=y_side if which == 0 else x_side,
            device_id_type=MESH,
        )

    def send_across(step, device, sem):
        chip = chip_at(order[step], 1 - y, 1 - x)
        return pltpu.make_async_remote_copy(
            src_ref=blocks.at[chip],
            dst_ref=blocks.at[chip],
            send_sem=sem,
            recv_sem=block_recv.at[chip],
            device_id=device,
            device_id_type=MESH,
        )

    def block_arrival(chip):
        pltpu.make_async_copy(blocks.at[chip], blocks.at[chip], block_recv.at[chip]).wait()

    def half_arrival(which, chip):
        place = blocks.at[chip, pl.ds(which * half, half)]
        pltpu.make_async_copy(place, place, half_recv.at[which, chip]).wait()

    def add_block(chip, source):
        local_tokens(chip).wait()
        sent_tokens(chip).wait_recv()
        part[...] += jnp.dot(tok[chip], source[...], preferred_element_type=jnp.float32)

    steps = len(order)
    for device, sem in ((x_side, x_send), (y_side, y_send), (pair_side, z_send)):
        send_block(0, device, sem).start()

    @pl.when(inner)
    def _():
        send_block(0, cross_side, cross_send).start()

    @pl.loop(0, chips)
    def _(chip):
        sent_tokens(chip).start()
        local_tokens(chip).start()

    part[...] = jnp.zeros_like(part)

    places_copy.wait()
    row = lax.broadcasted_iota(jnp.int32, (count, count), 0)
    lane = lax.broadcasted_iota(jnp.int32, (count, count), 1)
    places = jnp.sum(
        jnp.where(row == lane, places_ref[...].astype(jnp.float32), 0.0), axis=1, keepdims=True
    )
    cosine[...], sine[...] = rope_tables(places, head_dim)

    def rotate(values_in):
        return values_in * cosine[...] + pltpu.roll(values_in, head_dim // 2, 1) * sine[...]

    own_chip = chip_at(z, y, x)
    line = [chip_at(plane, y, x) for plane in order]
    along_x = [chip_at(plane, y, 1 - x) for plane in order]
    along_y = [chip_at(plane, 1 - y, x) for plane in order]
    corner = [chip_at(plane, 1 - y, 1 - x) for plane in order]

    def add_blocks(*chips_in):
        for chip in chips_in:
            add_block(chip, blocks.at[chip])

    def forward_halves(step):
        for which, chip in enumerate((along_x[step], along_y[step])):
            block_arrival(chip)
            send_half(step, which).start()

    def forward_line(step):
        block_arrival(line[step])

        @pl.when(inner)
        def _():
            if step == 1:
                send_block(step, cross_side, cross_send).start()
            else:
                send_block(step, pair_side, z_send).start()

        send_block(step, x_side, x_send).start()
        send_block(step, y_side, y_send).start()

    query_copy.wait()
    heads = query.shape[1] // head_dim
    add_block(own_chip, weight_ref)
    forward_halves(0)
    forward_line(1)
    forward_line(2)
    half_arrival(0, corner[0])
    half_arrival(1, corner[0])
    send_across(0, pair_side, across_send.at[0]).start()

    @pl.when(inner)
    def _():
        send_across(0, cross_side, across_send.at[1]).start()

    for head in range(heads):
        at = slice(head * head_dim, (head + 1) * head_dim)
        rotated[:, at] = rotate(query[:, at].astype(jnp.float32)).astype(jnp.bfloat16)
    forward_line(3)
    add_blocks(along_x[0], along_y[0], line[1])

    @pl.when(inner)
    def _():
        block_arrival(corner[2])
        send_across(2, pair_side, across_send.at[2]).start()

    add_blocks(line[2], corner[0])
    block_arrival(along_x[1])
    block_arrival(along_y[1])
    add_blocks(along_x[1], along_y[1])
    block_arrival(along_x[2])
    block_arrival(along_y[2])
    forward_halves(3)
    add_blocks(along_x[2], along_y[2], line[3], along_x[3], along_y[3])
    block_arrival(corner[1])
    add_blocks(corner[1])

    @pl.when((z == 0) | (z == 3))
    def _():
        block_arrival(corner[2])

    add_blocks(corner[2])
    half_arrival(0, corner[3])
    half_arrival(1, corner[3])
    add_blocks(corner[3])

    back_copy = pltpu.make_async_remote_copy(
        src_ref=part.at[rows_of(1 - core)],
        dst_ref=back,
        send_sem=back_sems.at[0],
        recv_sem=back_sems.at[1],
        device_id=peer,
        device_id_type=MESH,
    )
    back_copy.start()
    back_copy.wait_recv()
    projected = part[rows_of(core)] + back[...]
    own = pl.ds(2 * count, count)
    kv[own, :head_dim] = rotate(projected[:, :head_dim]).astype(jnp.bfloat16)
    kv[own, head_dim:] = projected[:, head_dim:].astype(jnp.bfloat16)

    def send_kv(distance):
        return pltpu.make_async_remote_copy(
            src_ref=kv.at[own],
            dst_ref=kv.at[pl.ds((2 - distance) * count, count)],
            send_sem=kv_send.at[distance - 1],
            recv_sem=kv_recv.at[distance - 1],
            device_id=ordinal(next_one if distance == 1 else next_two),
            device_id_type=MESH,
        )

    for distance in (1, 2):

        @pl.when(me < total - distance)
        def _():
            send_kv(distance).start()

        @pl.when(me < distance)
        def _():
            kv[pl.ds((2 - distance) * count, count), :] = jnp.zeros(
                (count, 2 * head_dim), jnp.bfloat16
            )

    near_limit = row - places.astype(jnp.int32)
    early = lax.broadcasted_iota(jnp.int32, (count, 2 * count), 1) - 2 * count
    allowed_own = (lane <= row) & (lane >= near_limit)
    allowed_early = early >= near_limit[:, :1]

    def score(head, keys, allowed):
        scores = lax.dot_general(
            rotated[:, head * head_dim : (head + 1) * head_dim],
            keys,
            (((1,), (1,)), ((), ())),
            preferred_element_type=jnp.float32,
        ) * head_dim ** (-0.5)
        return jnp.where(allowed, scores, masked_score)

    own_keys = kv[own, :head_dim]
    for head in range(heads):
        own_scores[head] = score(head, own_keys, allowed_own)

    for distance in (1, 2):

        @pl.when(me >= distance)
        def _():
            send_kv(distance).wait_recv()

    past = pl.ds(0, 2 * count)
    early_keys = kv[past, :head_dim]
    early_values = kv[past, head_dim:]
    own_values = kv[own, head_dim:]
    for head in range(heads):
        at = slice(head * head_dim, (head + 1) * head_dim)
        near = own_scores[head]
        far = score(head, early_keys, allowed_early)
        top = jnp.maximum(
            jnp.max(near, axis=1, keepdims=True), jnp.max(far, axis=1, keepdims=True)
        )
        near = jnp.exp(near - top)
        far = jnp.exp(far - top)
        share = 1.0 / (
            jnp.sum(near, axis=1, keepdims=True) + jnp.sum(far, axis=1, keepdims=True)
        )
        result = jnp.dot(
            (near * share).astype(jnp.bfloat16), own_values, preferred_element_type=jnp.float32
        ) + jnp.dot(
            (far * share).astype(jnp.bfloat16), early_values, preferred_element_type=jnp.float32
        )
        out_ref[:, at] = result.astype(jnp.bfloat16)

    for step in range(steps):
        send_block(step, x_side, x_send).wait_send()
        send_block(step, y_side, y_send).wait_send()
    for step in (0, 3):
        send_half(step, 0).wait_send()
        send_half(step, 1).wait_send()
    send_block(0, pair_side, z_send).wait_send()
    send_across(0, pair_side, across_send.at[0]).wait_send()

    @pl.when(inner)
    def _():
        send_block(2, pair_side, z_send).wait_send()
        send_block(3, pair_side, z_send).wait_send()
        send_block(0, cross_side, cross_send).wait_send()
        send_block(1, cross_side, cross_send).wait_send()
        send_across(0, cross_side, across_send.at[1]).wait_send()
        send_across(2, pair_side, across_send.at[2]).wait_send()

    @pl.loop(0, chips)
    def _(chip):
        sent_tokens(chip).wait_send()

    back_copy.wait_send()
    for distance in (1, 2):

        @pl.when(me < total - distance)
        def _():
            send_kv(distance).wait_send()


def fused_local(tokens, queries, positions, grad, master, moment1, moment2, step):
    new_master, new_first, new_second = adam_update(grad, master, moment1, moment2, step)
    weight = new_master.astype(jnp.bfloat16)
    count = tokens.shape[0]
    depth, width = weight.shape
    head_dim = width // 2
    chips = tokens.shape[1] // depth // 2
    dma = pltpu.SemaphoreType.DMA
    anywhere = pl.BlockSpec(memory_space=pl.ANY)
    inside = pl.BlockSpec(memory_space=pltpu.VMEM)
    attention = pl.pallas_call(
        fused_kernel,
        out_shape=jax.ShapeDtypeStruct(queries.shape, jnp.bfloat16),
        in_specs=[anywhere, anywhere, inside, anywhere],
        out_specs=inside,
        scratch_shapes=[
            pltpu.VMEM((1, count), jnp.int32),
            pltpu.VMEM((queries.shape[1] // head_dim, count, count), jnp.float32),
            pltpu.VMEM((chips, 2 * count, depth), jnp.bfloat16),
            pltpu.VMEM((chips, depth, width), jnp.bfloat16),
            pltpu.VMEM(queries.shape, jnp.bfloat16),
            pltpu.VMEM(queries.shape, jnp.bfloat16),
            pltpu.VMEM((2 * count, width), jnp.float32),
            pltpu.VMEM((count, width), jnp.float32),
            pltpu.VMEM((3 * count, width), jnp.bfloat16),
            pltpu.VMEM((count, head_dim), jnp.float32),
            pltpu.VMEM((count, head_dim), jnp.float32),
            dma((chips,)), dma((chips,)), dma((chips,)), dma, dma,
            dma((chips,)), dma((2, chips)),
            dma((4,)), dma((4,)), dma((4,)), dma((4,)), dma((4,)), dma((4,)), dma((3,)),
            dma((2,)), dma((2,)), dma((2,)),
        ],
        compiler_params=pltpu.CompilerParams(
            collective_id=0, has_side_effects=True, vmem_limit_bytes=63 * 1024 * 1024
        ),
    )(tokens, queries, weight, positions.reshape(1, -1))
    return (attention, new_master, new_first, new_second)


def solution(mesh):
    small = (mesh.shape["dp"], mesh.shape["seq"]) == (4, 8)
    return jax.shard_map(
        fused_local if small else local,
        mesh=mesh,
        in_specs=(
            P(("dp", "seq"), None),
            P(("dp", "seq"), None),
            P(("dp", "seq")),
            P(("dp", "seq"), None),
            P(("dp", "seq"), None),
            P(("dp", "seq"), None),
            P(("dp", "seq"), None),
            P(),
        ),
        out_specs=(
            P(("dp", "seq"), None),
            P(("dp", "seq"), None),
            P(("dp", "seq"), None),
            P(("dp", "seq"), None),
        ),
        check_vma=False,
    )
```

```python
import math

import jax
import jax.numpy as jnp
from jax import lax
from jax.experimental import pallas as pl
from jax.experimental.pallas import tpu as pltpu
from jax.sharding import PartitionSpec as P

GROUP = 8
MESH = pl.DeviceIdType.MESH


beta_one = 0.9
beta_two = 0.95
learn_rate = 0.02
adam_eps = 1e-08
rope_base = 500000.0
masked_score = -1e30


def shifted(value, axis, steps):
    count = lax.axis_size(axis)
    first, last = (max(0, -steps), min(count, count - steps))
    return lax.ppermute(value, axis, [(source, source + steps) for source in range(first, last)])


def rotate_pairs(values_in, places):
    half_width = values_in.shape[-1] // 2
    freqs = jnp.exp(
        jnp.arange(half_width, dtype=jnp.float32)
        * (-2.0 * math.log(rope_base) / values_in.shape[-1])
    )
    angles = places.astype(jnp.float32)[:, None, None] * freqs
    cosine = jnp.cos(angles)
    sine = jnp.sin(angles)
    first = values_in[..., :half_width]
    second = values_in[..., half_width:]
    return jnp.concatenate(
        [first * cosine - second * sine, second * cosine + first * sine], axis=-1
    )


def adam_update(grad, master, moment1, moment2, step):
    counter = step[0].astype(jnp.float32)
    new_first = beta_one * moment1 + (1.0 - beta_one) * grad
    new_second = beta_two * moment2 + (1.0 - beta_two) * grad * grad
    fixed_first = new_first / (1.0 - jnp.power(jnp.float32(beta_one), counter))
    fixed_second = new_second / (1.0 - jnp.power(jnp.float32(beta_two), counter))
    new_master = master - learn_rate * fixed_first / (jnp.sqrt(fixed_second) + adam_eps)
    return (new_master, new_first, new_second)


def attend_rows(query_rows, query_global, query_places, keys, values_v, key_global):
    row_count = query_rows.shape[0]
    block = 512

    def one_block(triple):
        rows, index, places = triple
        scores = jnp.einsum(
            "rd,kd->rk", rows, keys, preferred_element_type=jnp.float32
        ) * rows.shape[-1] ** (-0.5)
        allowed = (key_global[None, :] <= index[:, None]) & (
            key_global[None, :] >= (index - places)[:, None]
        )
        scores = jnp.where(allowed, scores, masked_score)
        top_score = jnp.max(scores, axis=1, keepdims=True)
        weights = jnp.exp(scores - top_score)
        totals = jnp.sum(weights, axis=1, keepdims=True)
        probs = (weights / totals).astype(jnp.bfloat16)
        return jnp.dot(probs, values_v, preferred_element_type=jnp.float32).astype(jnp.bfloat16)

    blocks = lax.map(
        one_block,
        (
            query_rows.reshape(-1, block, query_rows.shape[1]),
            query_global.reshape(-1, block),
            query_places.reshape(-1, block),
        ),
    )
    return blocks.reshape(row_count, -1)


def local(tokens, queries, positions, grad, master, moment1, moment2, step):
    new_master, new_first, new_second = adam_update(grad, master, moment1, moment2, step)
    weight = new_master.astype(jnp.bfloat16)
    head_dim = weight.shape[1] // 2
    local_count = tokens.shape[0]
    projected = jnp.dot(
        tokens,
        lax.all_gather(weight, ("dp", "seq"), axis=0, tiled=True),
        preferred_element_type=jnp.float32,
    )
    local_keys = rotate_pairs(projected[:, None, :head_dim], positions)[:, 0]
    key_value = jnp.concatenate([local_keys, projected[:, head_dim:]], axis=1).astype(jnp.bfloat16)
    group_kv = lax.all_gather(key_value, "seq", axis=0, tiled=True)
    span = group_kv.shape[0]
    reach = span // 4
    earlier = shifted(group_kv[span - reach :], "dp", 1)
    window = jnp.concatenate([earlier, group_kv], axis=0)
    group_index = lax.axis_index("dp")
    my_index = lax.axis_index("seq")
    window_start = group_index * span - reach
    rotated = rotate_pairs(
        queries.astype(jnp.float32).reshape(local_count, GROUP, head_dim), positions
    ).astype(jnp.bfloat16)
    offset = my_index * local_count
    near = lax.dynamic_slice_in_dim(window, offset, reach + local_count, 0)
    key_global = window_start + offset + jnp.arange(reach + local_count, dtype=jnp.int32)
    query_global = jnp.repeat(
        group_index * span + offset + jnp.arange(local_count, dtype=jnp.int32), GROUP
    )
    query_places = jnp.repeat(positions, GROUP)
    results = attend_rows(
        rotated.reshape(local_count * GROUP, head_dim),
        query_global,
        query_places,
        near[:, :head_dim],
        near[:, head_dim:],
        key_global,
    )
    attention = results.reshape(local_count, GROUP * head_dim)
    return (attention, new_master, new_first, new_second)


def rope_tables(places, width):
    lane = lax.broadcasted_iota(jnp.int32, (1, width), 1)
    half_width = width // 2
    slot = jnp.where(lane < half_width, lane, lane - half_width).astype(jnp.float32)
    freqs = jnp.exp(slot * (-2.0 * math.log(rope_base) / width))
    angles = places.astype(jnp.float32) * freqs
    sine = jnp.sin(angles)
    return jnp.cos(angles), jnp.where(lane < half_width, -sine, sine)


def fused_kernel(
    tok_hbm, query_hbm, weight_ref, places_hbm, out_ref,
    places_ref, own_scores, probs, tok, blocks, query, rotated, part, back, past_keys, past_values, cosine, sine,
    tok_sem, tok_send, tok_recv, query_sem, places_sem, piece_recv,
    x_send, y_send, z_send, cross_send, half_x_send, half_y_send, across_send,
    back_sems, kv_send, kv_recv,
):
    z = lax.axis_index("dp")
    seq = lax.axis_index("seq")
    planes = lax.axis_size("dp")
    wide = lax.axis_size("seq")
    core = lax.rem(seq, 2)
    x = lax.rem(seq // 2, 2)
    y = seq // 4
    count = tok_hbm.shape[0]
    depth = weight_ref.shape[0]
    half = depth // 2
    head_dim = weight_ref.shape[1] // 2
    me = z * wide + seq
    total = planes * wide
    chips = blocks.shape[0]

    def ordinal(index):
        return (index // wide, lax.rem(index, wide))

    peer = (z, seq + 1 - 2 * core)
    x_side = (z, seq + 2 - 4 * x)
    y_side = (z, seq + 4 - 8 * y)
    z_pair = z + 1 - 2 * lax.rem(z, 2)
    pair_side = (z_pair, seq)
    cross_side = (3 - z, seq)
    inner = (z == 1) | (z == 2)
    next_one, next_two = lax.rem(me + 1, total), lax.rem(me + 2, total)
    last_one, last_two = lax.rem(me + total - 1, total), lax.rem(me + total - 2, total)

    barrier = pltpu.get_barrier_semaphore()
    greeted = [peer, x_side, y_side, pair_side, cross_side]
    greeted += [ordinal(index) for index in (next_one, next_two, last_one, last_two)]
    for device in greeted:
        pl.semaphore_signal(barrier, inc=1, device_id=device, device_id_type=MESH)

    def columns(chip, which):
        return pl.ds(pl.multiple_of((chip * 2 + which) * depth, depth), depth)

    def rows_of(which):
        return pl.ds(pl.multiple_of(which * count, count), count)

    def local_tokens(chip):
        return pltpu.make_async_copy(
            tok_hbm.at[:, columns(chip, core)], tok.at[chip, rows_of(core)], tok_sem.at[chip]
        )

    def sent_tokens(chip):
        return pltpu.make_async_remote_copy(
            src_ref=tok_hbm.at[:, columns(chip, 1 - core)],
            dst_ref=tok.at[chip, rows_of(core)],
            send_sem=tok_send.at[chip],
            recv_sem=tok_recv.at[chip],
            device_id=peer,
            device_id_type=MESH,
        )

    query_copy = pltpu.make_async_copy(query_hbm, query, query_sem)
    places_copy = pltpu.make_async_copy(places_hbm, places_ref, places_sem)
    query_copy.start()
    places_copy.start()
    pl.semaphore_wait(barrier, len(greeted))

    order = [z, z_pair, 2 - z // 2, 3 - 3 * (z // 2)]

    def chip_at(plane, y_at, x_at):
        return plane * 4 + y_at * 2 + x_at

    spots = {"line": (y, x), "along_x": (y, 1 - x), "along_y": (1 - y, x), "corner": (1 - y, 1 - x)}

    def chip_of(kind, step):
        return chip_at(order[step], *spots[kind])

    def send_piece(kind, step, which, device, sem):
        chip = chip_of(kind, step)
        rows = pl.ds(which * half, half)
        own_block = kind == "line" and step == 0
        return pltpu.make_async_remote_copy(
            src_ref=weight_ref.at[rows] if own_block else blocks.at[chip, rows],
            dst_ref=blocks.at[chip, rows],
            send_sem=sem,
            recv_sem=piece_recv.at[which, chip],
            device_id=device,
            device_id_type=MESH,
        )

    def send_line(step, which, side):
        device, sem = {
            "x": (x_side, x_send),
            "y": (y_side, y_send),
            "pair": (pair_side, z_send),
            "cross": (cross_side, cross_send),
        }[side]
        return send_piece("line", step, which, device, sem.at[2 * step + which])

    def send_half(step, which):
        if which == 0:
            return send_piece("along_x", step, 0, y_side, half_y_send.at[step])
        return send_piece("along_y", step, 1, x_side, half_x_send.at[step])

    def send_corner(which, side):
        device, offset = {"pair": (pair_side, 0), "cross": (cross_side, 2)}[side]
        return send_piece("corner", 0, which, device, across_send.at[offset + which])

    arrived = set()

    def arrive(kind, step, which):
        if (kind, step, which) not in arrived:
            arrived.add((kind, step, which))
            chip = chip_of(kind, step)
            place = blocks.at[chip, pl.ds(which * half, half)]
            pltpu.make_async_copy(place, place, piece_recv.at[which, chip]).wait()

    def add_block(chip, source):
        local_tokens(chip).wait()
        sent_tokens(chip).wait_recv()
        part[...] += jnp.dot(tok[chip], source[...], preferred_element_type=jnp.float32)

    def add(kind, step):
        arrive(kind, step, 0)
        arrive(kind, step, 1)
        chip = chip_of(kind, step)
        add_block(chip, blocks.at[chip])

    steps = len(order)
    for which in range(2):
        for side in ("x", "y", "pair"):
            send_line(0, which, side).start()

        @pl.when(inner)
        def _():
            send_line(0, which, "cross").start()

    @pl.loop(0, chips)
    def _(chip):
        sent_tokens(chip).start()
        local_tokens(chip).start()

    part[...] = jnp.zeros_like(part)

    def rotate(values_in):
        return values_in * cosine[...] + pltpu.roll(values_in, head_dim // 2, 1) * sine[...]

    def forward_half(step, which):
        arrive("along_y" if which else "along_x", step, which)
        send_half(step, which).start()

    def forward_line(step, which):
        arrive("line", step, which)

        @pl.when(inner)
        def _():
            send_line(step, which, "cross" if step == 1 else "pair").start()

        send_line(step, which, "x").start()
        send_line(step, which, "y").start()

    forward_half(0, 0)
    forward_line(1, 0)
    forward_half(0, 1)
    forward_line(1, 1)
    add_block(chip_of("line", 0), weight_ref)
    forward_line(2, 0)
    forward_line(2, 1)
    for which in range(2):
        arrive("corner", 0, which)
        send_corner(which, "pair").start()

        @pl.when(inner)
        def _():
            send_corner(which, "cross").start()

    add("line", 1)
    add("along_x", 0)
    add("along_y", 0)
    forward_line(3, 0)
    forward_line(3, 1)

    places_copy.wait()
    row = lax.broadcasted_iota(jnp.int32, (count, count), 0)
    lane = lax.broadcasted_iota(jnp.int32, (count, count), 1)
    places = jnp.sum(
        jnp.where(row == lane, places_ref[...].astype(jnp.float32), 0.0), axis=1, keepdims=True
    )
    cosine[...], sine[...] = rope_tables(places, head_dim)
    add("corner", 0)
    add("line", 2)
    add("along_x", 1)
    add("along_y", 1)
    outer = (z == 0) | (z == 3)
    for which in range(2):
        arrive("along_y" if which else "along_x", 2, which)

        @pl.when(outer)
        def _():
            send_half(2, which).start()

    query_copy.wait()
    heads = query.shape[1] // head_dim
    for head in range(heads):
        at = slice(head * head_dim, (head + 1) * head_dim)
        rotated[:, at] = rotate(query[:, at].astype(jnp.float32)).astype(jnp.bfloat16)
    add("line", 3)
    forward_half(3, 0)
    forward_half(3, 1)
    add("along_x", 2)
    add("along_y", 2)
    add("corner", 1)
    add("along_x", 3)
    add("along_y", 3)
    add("corner", 2)
    add("corner", 3)

    sides = (pl.ds(0, head_dim), pl.ds(head_dim, head_dim))

    def back_copy(side):
        return pltpu.make_async_remote_copy(
            src_ref=part.at[rows_of(1 - core), sides[side]],
            dst_ref=back.at[:, sides[side]],
            send_sem=back_sems.at[0, side],
            recv_sem=back_sems.at[1, side],
            device_id=peer,
            device_id_type=MESH,
        )

    own = pl.ds(2 * count, count)
    pasts = (past_keys, past_values)

    def send_past(side, distance):
        return pltpu.make_async_remote_copy(
            src_ref=pasts[side].at[own],
            dst_ref=pasts[side].at[pl.ds((2 - distance) * count, count)],
            send_sem=kv_send.at[side, distance - 1],
            recv_sem=kv_recv.at[side, distance - 1],
            device_id=ordinal(next_one if distance == 1 else next_two),
            device_id_type=MESH,
        )

    back_copy(0).start()
    back_copy(1).start()
    for side in range(2):
        back_copy(side).wait_recv()
        projected = part[rows_of(core), sides[side]] + back[:, sides[side]]
        if side == 0:
            projected = rotate(projected)
        pasts[side][own, :] = projected.astype(jnp.bfloat16)
        for distance in (2, 1):

            @pl.when(me < total - distance)
            def _():
                send_past(side, distance).start()

            @pl.when(me < distance)
            def _():
                pasts[side][pl.ds((2 - distance) * count, count), :] = jnp.zeros(
                    (count, head_dim), jnp.bfloat16
                )

    def past_arrival(side):
        for distance in (1, 2):

            @pl.when(me >= distance)
            def _():
                send_past(side, distance).wait_recv()

    near_limit = row - places.astype(jnp.int32)
    early = lax.broadcasted_iota(jnp.int32, (count, 2 * count), 1) - 2 * count
    allowed_own = (lane <= row) & (lane >= near_limit)
    allowed_early = early >= near_limit[:, :1]

    def score(head, keys, allowed):
        scores = lax.dot_general(
            rotated[:, head * head_dim : (head + 1) * head_dim],
            keys,
            (((1,), (1,)), ((), ())),
            preferred_element_type=jnp.float32,
        ) * head_dim ** (-0.5)
        return jnp.where(allowed, scores, masked_score)

    own_keys = past_keys[own, :]
    for head in range(heads):
        own_scores[head] = score(head, own_keys, allowed_own)

    past = pl.ds(0, 2 * count)
    past_arrival(0)
    early_keys = past_keys[past, :]
    for head in range(heads):
        near = own_scores[head]
        far = score(head, early_keys, allowed_early)
        top = jnp.maximum(
            jnp.max(near, axis=1, keepdims=True), jnp.max(far, axis=1, keepdims=True)
        )
        near = jnp.exp(near - top)
        far = jnp.exp(far - top)
        share = 1.0 / (
            jnp.sum(near, axis=1, keepdims=True) + jnp.sum(far, axis=1, keepdims=True)
        )
        probs[head, :, : 2 * count] = (far * share).astype(jnp.bfloat16)
        probs[head, :, 2 * count :] = (near * share).astype(jnp.bfloat16)
    past_arrival(1)
    values_v = past_values[...]
    for head in range(heads):
        out_ref[:, head * head_dim : (head + 1) * head_dim] = jnp.dot(
            probs[head], values_v, preferred_element_type=jnp.float32
        ).astype(jnp.bfloat16)

    for which in range(2):
        for step in range(steps):
            send_line(step, which, "x").wait_send()
            send_line(step, which, "y").wait_send()
        send_half(0, which).wait_send()
        send_half(3, which).wait_send()
        send_line(0, which, "pair").wait_send()
        send_corner(which, "pair").wait_send()

        @pl.when(outer)
        def _():
            send_half(2, which).wait_send()

        @pl.when(inner)
        def _():
            send_line(2, which, "pair").wait_send()
            send_line(3, which, "pair").wait_send()
            send_line(0, which, "cross").wait_send()
            send_line(1, which, "cross").wait_send()
            send_corner(which, "cross").wait_send()

    @pl.loop(0, chips)
    def _(chip):
        sent_tokens(chip).wait_send()

    for side in range(2):
        back_copy(side).wait_send()
        for distance in (1, 2):

            @pl.when(me < total - distance)
            def _():
                send_past(side, distance).wait_send()


def fused_local(tokens, queries, positions, grad, master, moment1, moment2, step):
    new_master, new_first, new_second = adam_update(grad, master, moment1, moment2, step)
    weight = new_master.astype(jnp.bfloat16)
    count = tokens.shape[0]
    depth, width = weight.shape
    head_dim = width // 2
    chips = tokens.shape[1] // depth // 2
    dma = pltpu.SemaphoreType.DMA
    anywhere = pl.BlockSpec(memory_space=pl.ANY)
    inside = pl.BlockSpec(memory_space=pltpu.VMEM)
    attention = pl.pallas_call(
        fused_kernel,
        out_shape=jax.ShapeDtypeStruct(queries.shape, jnp.bfloat16),
        in_specs=[anywhere, anywhere, inside, anywhere],
        out_specs=inside,
        scratch_shapes=[
            pltpu.VMEM((1, count), jnp.int32),
            pltpu.VMEM((queries.shape[1] // head_dim, count, count), jnp.float32),
            pltpu.VMEM((queries.shape[1] // head_dim, count, 3 * count), jnp.bfloat16),
            pltpu.VMEM((chips, 2 * count, depth), jnp.bfloat16),
            pltpu.VMEM((chips, depth, width), jnp.bfloat16),
            pltpu.VMEM(queries.shape, jnp.bfloat16),
            pltpu.VMEM(queries.shape, jnp.bfloat16),
            pltpu.VMEM((2 * count, width), jnp.float32),
            pltpu.VMEM((count, width), jnp.float32),
            pltpu.VMEM((3 * count, head_dim), jnp.bfloat16),
            pltpu.VMEM((3 * count, head_dim), jnp.bfloat16),
            pltpu.VMEM((count, head_dim), jnp.float32),
            pltpu.VMEM((count, head_dim), jnp.float32),
            dma((chips,)), dma((chips,)), dma((chips,)), dma, dma,
            dma((2, chips)),
            dma((8,)), dma((8,)), dma((8,)), dma((4,)), dma((4,)), dma((4,)), dma((4,)),
            dma((2, 2)), dma((2, 2)), dma((2, 2)),
        ],
        compiler_params=pltpu.CompilerParams(
            collective_id=0, has_side_effects=True, vmem_limit_bytes=62 * 1024 * 1024
        ),
    )(tokens, queries, weight, positions.reshape(1, -1))
    return (attention, new_master, new_first, new_second)


def solution(mesh):
    small = (mesh.shape["dp"], mesh.shape["seq"]) == (4, 8)
    return jax.shard_map(
        fused_local if small else local,
        mesh=mesh,
        in_specs=(
            P(("dp", "seq"), None),
            P(("dp", "seq"), None),
            P(("dp", "seq")),
            P(("dp", "seq"), None),
            P(("dp", "seq"), None),
            P(("dp", "seq"), None),
            P(("dp", "seq"), None),
            P(),
        ),
        out_specs=(
            P(("dp", "seq"), None),
            P(("dp", "seq"), None),
            P(("dp", "seq"), None),
            P(("dp", "seq"), None),
        ),
        check_vma=False,
    )
```

```python
import math

import jax
import jax.numpy as jnp
from jax import lax
from jax.experimental import pallas as pl
from jax.experimental.pallas import tpu as pltpu
from jax.sharding import PartitionSpec as P

GROUP = 8
MESH = pl.DeviceIdType.MESH


beta_one = 0.9
beta_two = 0.95
learn_rate = 0.02
adam_eps = 1e-08
rope_base = 500000.0
masked_score = -1e30


def shifted(value, axis, steps):
    count = lax.axis_size(axis)
    first, last = (max(0, -steps), min(count, count - steps))
    return lax.ppermute(value, axis, [(source, source + steps) for source in range(first, last)])


def rotate_pairs(values_in, places):
    half_width = values_in.shape[-1] // 2
    freqs = jnp.exp(
        jnp.arange(half_width, dtype=jnp.float32)
        * (-2.0 * math.log(rope_base) / values_in.shape[-1])
    )
    angles = places.astype(jnp.float32)[:, None, None] * freqs
    cosine = jnp.cos(angles)
    sine = jnp.sin(angles)
    first = values_in[..., :half_width]
    second = values_in[..., half_width:]
    return jnp.concatenate(
        [first * cosine - second * sine, second * cosine + first * sine], axis=-1
    )


def adam_update(grad, master, moment1, moment2, step):
    counter = step[0].astype(jnp.float32)
    new_first = beta_one * moment1 + (1.0 - beta_one) * grad
    new_second = beta_two * moment2 + (1.0 - beta_two) * grad * grad
    fixed_first = new_first / (1.0 - jnp.power(jnp.float32(beta_one), counter))
    fixed_second = new_second / (1.0 - jnp.power(jnp.float32(beta_two), counter))
    new_master = master - learn_rate * fixed_first / (jnp.sqrt(fixed_second) + adam_eps)
    return (new_master, new_first, new_second)


def attend_rows(query_rows, query_global, query_places, keys, values_v, key_global):
    row_count = query_rows.shape[0]
    block = 512

    def one_block(triple):
        rows, index, places = triple
        scores = jnp.einsum(
            "rd,kd->rk", rows, keys, preferred_element_type=jnp.float32
        ) * rows.shape[-1] ** (-0.5)
        allowed = (key_global[None, :] <= index[:, None]) & (
            key_global[None, :] >= (index - places)[:, None]
        )
        scores = jnp.where(allowed, scores, masked_score)
        top_score = jnp.max(scores, axis=1, keepdims=True)
        weights = jnp.exp(scores - top_score)
        totals = jnp.sum(weights, axis=1, keepdims=True)
        probs = (weights / totals).astype(jnp.bfloat16)
        return jnp.dot(probs, values_v, preferred_element_type=jnp.float32).astype(jnp.bfloat16)

    blocks = lax.map(
        one_block,
        (
            query_rows.reshape(-1, block, query_rows.shape[1]),
            query_global.reshape(-1, block),
            query_places.reshape(-1, block),
        ),
    )
    return blocks.reshape(row_count, -1)


def local(tokens, queries, positions, grad, master, moment1, moment2, step):
    new_master, new_first, new_second = adam_update(grad, master, moment1, moment2, step)
    weight = new_master.astype(jnp.bfloat16)
    head_dim = weight.shape[1] // 2
    local_count = tokens.shape[0]
    projected = jnp.dot(
        tokens,
        lax.all_gather(weight, ("dp", "seq"), axis=0, tiled=True),
        preferred_element_type=jnp.float32,
    )
    local_keys = rotate_pairs(projected[:, None, :head_dim], positions)[:, 0]
    key_value = jnp.concatenate([local_keys, projected[:, head_dim:]], axis=1).astype(jnp.bfloat16)
    group_kv = lax.all_gather(key_value, "seq", axis=0, tiled=True)
    span = group_kv.shape[0]
    reach = span // 4
    earlier = shifted(group_kv[span - reach :], "dp", 1)
    window = jnp.concatenate([earlier, group_kv], axis=0)
    group_index = lax.axis_index("dp")
    my_index = lax.axis_index("seq")
    window_start = group_index * span - reach
    rotated = rotate_pairs(
        queries.astype(jnp.float32).reshape(local_count, GROUP, head_dim), positions
    ).astype(jnp.bfloat16)
    offset = my_index * local_count
    near = lax.dynamic_slice_in_dim(window, offset, reach + local_count, 0)
    key_global = window_start + offset + jnp.arange(reach + local_count, dtype=jnp.int32)
    query_global = jnp.repeat(
        group_index * span + offset + jnp.arange(local_count, dtype=jnp.int32), GROUP
    )
    query_places = jnp.repeat(positions, GROUP)
    results = attend_rows(
        rotated.reshape(local_count * GROUP, head_dim),
        query_global,
        query_places,
        near[:, :head_dim],
        near[:, head_dim:],
        key_global,
    )
    attention = results.reshape(local_count, GROUP * head_dim)
    return (attention, new_master, new_first, new_second)


def rope_tables(places, width):
    lane = lax.broadcasted_iota(jnp.int32, (1, width), 1)
    half_width = width // 2
    slot = jnp.where(lane < half_width, lane, lane - half_width).astype(jnp.float32)
    freqs = jnp.exp(slot * (-2.0 * math.log(rope_base) / width))
    angles = places.astype(jnp.float32) * freqs
    sine = jnp.sin(angles)
    return jnp.cos(angles), jnp.where(lane < half_width, -sine, sine)


def fused_kernel(
    tok_hbm, query_hbm, weight_ref, places_hbm, out_ref,
    places_ref, own_scores, probs, tok, blocks, query, rotated, part, back, past_keys, past_values, places, cosine, sine,
    tok_sem, tok_send, tok_recv, query_sem, places_sem, piece_recv,
    x_send, y_send, z_send, cross_send, half_x_send, half_y_send, across_send,
    back_sems, kv_send, kv_recv,
):
    z = lax.axis_index("dp")
    seq = lax.axis_index("seq")
    planes = lax.axis_size("dp")
    wide = lax.axis_size("seq")
    core = lax.rem(seq, 2)
    x = lax.rem(seq // 2, 2)
    y = seq // 4
    count = tok_hbm.shape[0]
    depth = weight_ref.shape[0]
    half = depth // 2
    head_dim = weight_ref.shape[1] // 2
    me = z * wide + seq
    total = planes * wide
    chips = blocks.shape[0]

    def ordinal(index):
        return (index // wide, lax.rem(index, wide))

    peer = (z, seq + 1 - 2 * core)
    x_side = (z, seq + 2 - 4 * x)
    y_side = (z, seq + 4 - 8 * y)
    z_pair = z + 1 - 2 * lax.rem(z, 2)
    pair_side = (z_pair, seq)
    cross_side = (3 - z, seq)
    inner = (z == 1) | (z == 2)
    next_one, next_two = lax.rem(me + 1, total), lax.rem(me + 2, total)
    last_one, last_two = lax.rem(me + total - 1, total), lax.rem(me + total - 2, total)

    barrier = pltpu.get_barrier_semaphore()
    greeted = [peer, x_side, y_side, pair_side, cross_side]
    greeted += [ordinal(index) for index in (next_one, next_two, last_one, last_two)]
    for device in greeted:
        pl.semaphore_signal(barrier, inc=1, device_id=device, device_id_type=MESH)

    def columns(chip, which):
        return pl.ds(pl.multiple_of((chip * 2 + which) * depth, depth), depth)

    def rows_of(which):
        return pl.ds(pl.multiple_of(which * count, count), count)

    def local_tokens(chip):
        return pltpu.make_async_copy(
            tok_hbm.at[:, columns(chip, core)], tok.at[chip, rows_of(core)], tok_sem.at[chip]
        )

    def sent_tokens(chip):
        return pltpu.make_async_remote_copy(
            src_ref=tok_hbm.at[:, columns(chip, 1 - core)],
            dst_ref=tok.at[chip, rows_of(core)],
            send_sem=tok_send.at[chip],
            recv_sem=tok_recv.at[chip],
            device_id=peer,
            device_id_type=MESH,
        )

    query_copy = pltpu.make_async_copy(query_hbm, query, query_sem)
    places_copy = pltpu.make_async_copy(places_hbm, places_ref, places_sem)
    query_copy.start()
    places_copy.start()
    pl.semaphore_wait(barrier, len(greeted))

    order = [z, z_pair, 2 - z // 2, 3 - 3 * (z // 2)]

    def chip_at(plane, y_at, x_at):
        return plane * 4 + y_at * 2 + x_at

    spots = {"line": (y, x), "along_x": (y, 1 - x), "along_y": (1 - y, x), "corner": (1 - y, 1 - x)}

    def chip_of(kind, step):
        return chip_at(order[step], *spots[kind])

    def send_piece(kind, step, which, device, sem):
        chip = chip_of(kind, step)
        rows = pl.ds(which * half, half)
        own_block = kind == "line" and step == 0
        return pltpu.make_async_remote_copy(
            src_ref=weight_ref.at[rows] if own_block else blocks.at[chip, rows],
            dst_ref=blocks.at[chip, rows],
            send_sem=sem,
            recv_sem=piece_recv.at[which, chip],
            device_id=device,
            device_id_type=MESH,
        )

    def send_line(step, which, side):
        device, sem = {
            "x": (x_side, x_send),
            "y": (y_side, y_send),
            "pair": (pair_side, z_send),
            "cross": (cross_side, cross_send),
        }[side]
        return send_piece("line", step, which, device, sem.at[2 * step + which])

    def send_half(step, which):
        if which == 0:
            return send_piece("along_x", step, 0, y_side, half_y_send.at[step])
        return send_piece("along_y", step, 1, x_side, half_x_send.at[step])

    def send_corner(which, side):
        device, offset = {"pair": (pair_side, 0), "cross": (cross_side, 2)}[side]
        return send_piece("corner", 0, which, device, across_send.at[offset + which])

    arrived = set()

    def arrive(kind, step, which):
        if (kind, step, which) not in arrived:
            arrived.add((kind, step, which))
            chip = chip_of(kind, step)
            place = blocks.at[chip, pl.ds(which * half, half)]
            pltpu.make_async_copy(place, place, piece_recv.at[which, chip]).wait()

    def add_block(chip, source):
        local_tokens(chip).wait()
        sent_tokens(chip).wait_recv()
        part[...] += jnp.dot(tok[chip], source[...], preferred_element_type=jnp.float32)

    def add(kind, step):
        arrive(kind, step, 0)
        arrive(kind, step, 1)
        chip = chip_of(kind, step)
        add_block(chip, blocks.at[chip])

    steps = len(order)
    for which in range(2):
        for side in ("x", "y", "pair"):
            send_line(0, which, side).start()

        @pl.when(inner)
        def _():
            send_line(0, which, "cross").start()

    @pl.loop(0, chips)
    def _(chip):
        sent_tokens(chip).start()
        local_tokens(chip).start()

    part[...] = jnp.zeros_like(part)

    def rotate(values_in):
        return values_in * cosine[...] + pltpu.roll(values_in, head_dim // 2, 1) * sine[...]

    def forward_half(step, which):
        arrive("along_y" if which else "along_x", step, which)
        send_half(step, which).start()

    def forward_line(step, which, onward=None):
        arrive("line", step, which)
        if onward is not None:
            send_line(step, which, onward).start()
        send_line(step, which, "x").start()
        send_line(step, which, "y").start()

    row = lax.broadcasted_iota(jnp.int32, (count, count), 0)
    lane = lax.broadcasted_iota(jnp.int32, (count, count), 1)
    heads = query.shape[1] // head_dim

    def prepare():
        places_copy.wait()
        places[...] = jnp.sum(
            jnp.where(row == lane, places_ref[...].astype(jnp.float32), 0.0),
            axis=1,
            keepdims=True,
        )
        cosine[...], sine[...] = rope_tables(places[...], head_dim)
        query_copy.wait()
        for head in range(heads):
            at = slice(head * head_dim, (head + 1) * head_dim)
            rotated[:, at] = rotate(query[:, at].astype(jnp.float32)).astype(jnp.bfloat16)

    outer = (z == 0) | (z == 3)

    @pl.when(inner)
    def _():
        arrived.clear()
        for which in range(2):
            forward_half(0, which)
            forward_line(1, which, "cross")
            forward_line(2, which, "pair")
        add_block(chip_of("line", 0), weight_ref)
        for which in range(2):
            arrive("corner", 0, which)
            send_corner(which, "cross").start()
        for which in range(2):
            forward_line(3, which, "pair")
        for which in range(2):
            send_corner(which, "pair").start()
        for item in (("along_x", 0), ("along_y", 0), ("line", 1), ("line", 2), ("corner", 0)):
            add(*item)
        prepare()
        for item in (("along_x", 1), ("along_y", 1), ("along_x", 2), ("along_y", 2)):
            add(*item)
        forward_half(3, 0)
        forward_half(3, 1)
        for item in (("line", 3), ("corner", 1), ("along_x", 3), ("along_y", 3)):
            add(*item)
        add("corner", 2)
        add("corner", 3)

    @pl.when(outer)
    def _():
        arrived.clear()
        for which in range(2):
            forward_half(0, which)
            forward_line(1, which)
        add_block(chip_of("line", 0), weight_ref)
        for which in range(2):
            arrive("corner", 0, which)
            send_corner(which, "pair").start()
        forward_line(2, 0)
        forward_line(2, 1)
        for item in (("along_x", 0), ("along_y", 0), ("line", 1), ("corner", 0)):
            add(*item)
        forward_line(3, 0)
        forward_line(3, 1)
        prepare()
        for item in (("along_x", 1), ("along_y", 1), ("line", 2)):
            add(*item)
        forward_half(2, 0)
        forward_half(2, 1)
        add("along_x", 2)
        add("along_y", 2)
        forward_half(3, 0)
        forward_half(3, 1)
        for item in (("line", 3), ("corner", 1), ("along_x", 3), ("along_y", 3)):
            add(*item)
        add("corner", 2)
        add("corner", 3)

    sides = (pl.ds(0, head_dim), pl.ds(head_dim, head_dim))

    def back_copy(side):
        return pltpu.make_async_remote_copy(
            src_ref=part.at[rows_of(1 - core), sides[side]],
            dst_ref=back.at[:, sides[side]],
            send_sem=back_sems.at[0, side],
            recv_sem=back_sems.at[1, side],
            device_id=peer,
            device_id_type=MESH,
        )

    own = pl.ds(2 * count, count)
    pasts = (past_keys, past_values)

    def send_past(side, distance):
        return pltpu.make_async_remote_copy(
            src_ref=pasts[side].at[own],
            dst_ref=pasts[side].at[pl.ds((2 - distance) * count, count)],
            send_sem=kv_send.at[side, distance - 1],
            recv_sem=kv_recv.at[side, distance - 1],
            device_id=ordinal(next_one if distance == 1 else next_two),
            device_id_type=MESH,
        )

    back_copy(0).start()
    back_copy(1).start()
    for side in range(2):
        back_copy(side).wait_recv()
        projected = part[rows_of(core), sides[side]] + back[:, sides[side]]
        if side == 0:
            projected = rotate(projected)
        pasts[side][own, :] = projected.astype(jnp.bfloat16)
        for distance in (2, 1):

            @pl.when(me < total - distance)
            def _():
                send_past(side, distance).start()

            @pl.when(me < distance)
            def _():
                pasts[side][pl.ds((2 - distance) * count, count), :] = jnp.zeros(
                    (count, head_dim), jnp.bfloat16
                )

    def past_arrival(side):
        for distance in (1, 2):

            @pl.when(me >= distance)
            def _():
                send_past(side, distance).wait_recv()

    near_limit = row - places[...].astype(jnp.int32)
    early = lax.broadcasted_iota(jnp.int32, (count, 2 * count), 1) - 2 * count
    allowed_own = (lane <= row) & (lane >= near_limit)
    allowed_early = early >= near_limit[:, :1]

    def score(head, keys, allowed):
        scores = lax.dot_general(
            rotated[:, head * head_dim : (head + 1) * head_dim],
            keys,
            (((1,), (1,)), ((), ())),
            preferred_element_type=jnp.float32,
        ) * head_dim ** (-0.5)
        return jnp.where(allowed, scores, masked_score)

    own_keys = past_keys[own, :]
    for head in range(heads):
        own_scores[head] = score(head, own_keys, allowed_own)

    past = pl.ds(0, 2 * count)
    past_arrival(0)
    early_keys = past_keys[past, :]
    for head in range(heads):
        near = own_scores[head]
        far = score(head, early_keys, allowed_early)
        top = jnp.maximum(
            jnp.max(near, axis=1, keepdims=True), jnp.max(far, axis=1, keepdims=True)
        )
        near = jnp.exp(near - top)
        far = jnp.exp(far - top)
        share = 1.0 / (
            jnp.sum(near, axis=1, keepdims=True) + jnp.sum(far, axis=1, keepdims=True)
        )
        probs[head, :, : 2 * count] = (far * share).astype(jnp.bfloat16)
        probs[head, :, 2 * count :] = (near * share).astype(jnp.bfloat16)
    past_arrival(1)
    values_v = past_values[...]
    for head in range(heads):
        out_ref[:, head * head_dim : (head + 1) * head_dim] = jnp.dot(
            probs[head], values_v, preferred_element_type=jnp.float32
        ).astype(jnp.bfloat16)

    for which in range(2):
        for step in range(steps):
            send_line(step, which, "x").wait_send()
            send_line(step, which, "y").wait_send()
        send_half(0, which).wait_send()
        send_half(3, which).wait_send()
        send_line(0, which, "pair").wait_send()
        send_corner(which, "pair").wait_send()

        @pl.when(outer)
        def _():
            send_half(2, which).wait_send()

        @pl.when(inner)
        def _():
            send_line(2, which, "pair").wait_send()
            send_line(3, which, "pair").wait_send()
            send_line(0, which, "cross").wait_send()
            send_line(1, which, "cross").wait_send()
            send_corner(which, "cross").wait_send()

    @pl.loop(0, chips)
    def _(chip):
        sent_tokens(chip).wait_send()

    for side in range(2):
        back_copy(side).wait_send()
        for distance in (1, 2):

            @pl.when(me < total - distance)
            def _():
                send_past(side, distance).wait_send()


def fused_local(tokens, queries, positions, grad, master, moment1, moment2, step):
    new_master, new_first, new_second = adam_update(grad, master, moment1, moment2, step)
    weight = new_master.astype(jnp.bfloat16)
    count = tokens.shape[0]
    depth, width = weight.shape
    head_dim = width // 2
    chips = tokens.shape[1] // depth // 2
    dma = pltpu.SemaphoreType.DMA
    anywhere = pl.BlockSpec(memory_space=pl.ANY)
    inside = pl.BlockSpec(memory_space=pltpu.VMEM)
    attention = pl.pallas_call(
        fused_kernel,
        out_shape=jax.ShapeDtypeStruct(queries.shape, jnp.bfloat16),
        in_specs=[anywhere, anywhere, inside, anywhere],
        out_specs=inside,
        scratch_shapes=[
            pltpu.VMEM((1, count), jnp.int32),
            pltpu.VMEM((queries.shape[1] // head_dim, count, count), jnp.float32),
            pltpu.VMEM((queries.shape[1] // head_dim, count, 3 * count), jnp.bfloat16),
            pltpu.VMEM((chips, 2 * count, depth), jnp.bfloat16),
            pltpu.VMEM((chips, depth, width), jnp.bfloat16),
            pltpu.VMEM(queries.shape, jnp.bfloat16),
            pltpu.VMEM(queries.shape, jnp.bfloat16),
            pltpu.VMEM((2 * count, width), jnp.float32),
            pltpu.VMEM((count, width), jnp.float32),
            pltpu.VMEM((3 * count, head_dim), jnp.bfloat16),
            pltpu.VMEM((3 * count, head_dim), jnp.bfloat16),
            pltpu.VMEM((count, 1), jnp.float32),
            pltpu.VMEM((count, head_dim), jnp.float32),
            pltpu.VMEM((count, head_dim), jnp.float32),
            dma((chips,)), dma((chips,)), dma((chips,)), dma, dma,
            dma((2, chips)),
            dma((8,)), dma((8,)), dma((8,)), dma((4,)), dma((4,)), dma((4,)), dma((4,)),
            dma((2, 2)), dma((2, 2)), dma((2, 2)),
        ],
        compiler_params=pltpu.CompilerParams(
            collective_id=0, has_side_effects=True, vmem_limit_bytes=121 * 512 * 1024
        ),
    )(tokens, queries, weight, positions.reshape(1, -1))
    return (attention, new_master, new_first, new_second)


def solution(mesh):
    small = (mesh.shape["dp"], mesh.shape["seq"]) == (4, 8)
    return jax.shard_map(
        fused_local if small else local,
        mesh=mesh,
        in_specs=(
            P(("dp", "seq"), None),
            P(("dp", "seq"), None),
            P(("dp", "seq")),
            P(("dp", "seq"), None),
            P(("dp", "seq"), None),
            P(("dp", "seq"), None),
            P(("dp", "seq"), None),
            P(),
        ),
        out_specs=(
            P(("dp", "seq"), None),
            P(("dp", "seq"), None),
            P(("dp", "seq"), None),
            P(("dp", "seq"), None),
        ),
        check_vma=False,
    )
```

```python
import math

import jax
import jax.numpy as jnp
from jax import lax
from jax.experimental import pallas as pl
from jax.experimental.pallas import tpu as pltpu
from jax.sharding import PartitionSpec as P

GROUP = 8
MESH = pl.DeviceIdType.MESH


beta_one = 0.9
beta_two = 0.95
learn_rate = 0.02
adam_eps = 1e-08
rope_base = 500000.0
masked_score = -1e30


def shifted(value, axis, steps):
    count = lax.axis_size(axis)
    first, last = (max(0, -steps), min(count, count - steps))
    return lax.ppermute(value, axis, [(source, source + steps) for source in range(first, last)])


def rotate_pairs(values_in, places):
    half_width = values_in.shape[-1] // 2
    freqs = jnp.exp(
        jnp.arange(half_width, dtype=jnp.float32)
        * (-2.0 * math.log(rope_base) / values_in.shape[-1])
    )
    angles = places.astype(jnp.float32)[:, None, None] * freqs
    cosine = jnp.cos(angles)
    sine = jnp.sin(angles)
    first = values_in[..., :half_width]
    second = values_in[..., half_width:]
    return jnp.concatenate(
        [first * cosine - second * sine, second * cosine + first * sine], axis=-1
    )


def adam_update(grad, master, moment1, moment2, step):
    counter = step[0].astype(jnp.float32)
    new_first = beta_one * moment1 + (1.0 - beta_one) * grad
    new_second = beta_two * moment2 + (1.0 - beta_two) * grad * grad
    fixed_first = new_first / (1.0 - jnp.power(jnp.float32(beta_one), counter))
    fixed_second = new_second / (1.0 - jnp.power(jnp.float32(beta_two), counter))
    new_master = master - learn_rate * fixed_first / (jnp.sqrt(fixed_second) + adam_eps)
    return (new_master, new_first, new_second)


def attend_rows(query_rows, query_global, query_places, keys, values_v, key_global):
    row_count = query_rows.shape[0]
    block = 512

    def one_block(triple):
        rows, index, places = triple
        scores = jnp.einsum(
            "rd,kd->rk", rows, keys, preferred_element_type=jnp.float32
        ) * rows.shape[-1] ** (-0.5)
        allowed = (key_global[None, :] <= index[:, None]) & (
            key_global[None, :] >= (index - places)[:, None]
        )
        scores = jnp.where(allowed, scores, masked_score)
        top_score = jnp.max(scores, axis=1, keepdims=True)
        weights = jnp.exp(scores - top_score)
        totals = jnp.sum(weights, axis=1, keepdims=True)
        probs = (weights / totals).astype(jnp.bfloat16)
        return jnp.dot(probs, values_v, preferred_element_type=jnp.float32).astype(jnp.bfloat16)

    blocks = lax.map(
        one_block,
        (
            query_rows.reshape(-1, block, query_rows.shape[1]),
            query_global.reshape(-1, block),
            query_places.reshape(-1, block),
        ),
    )
    return blocks.reshape(row_count, -1)


def local(tokens, queries, positions, grad, master, moment1, moment2, step):
    new_master, new_first, new_second = adam_update(grad, master, moment1, moment2, step)
    weight = new_master.astype(jnp.bfloat16)
    head_dim = weight.shape[1] // 2
    local_count = tokens.shape[0]
    projected = jnp.dot(
        tokens,
        lax.all_gather(weight, ("dp", "seq"), axis=0, tiled=True),
        preferred_element_type=jnp.float32,
    )
    local_keys = rotate_pairs(projected[:, None, :head_dim], positions)[:, 0]
    key_value = jnp.concatenate([local_keys, projected[:, head_dim:]], axis=1).astype(jnp.bfloat16)
    group_kv = lax.all_gather(key_value, "seq", axis=0, tiled=True)
    span = group_kv.shape[0]
    reach = span // 4
    earlier = shifted(group_kv[span - reach :], "dp", 1)
    window = jnp.concatenate([earlier, group_kv], axis=0)
    group_index = lax.axis_index("dp")
    my_index = lax.axis_index("seq")
    window_start = group_index * span - reach
    rotated = rotate_pairs(
        queries.astype(jnp.float32).reshape(local_count, GROUP, head_dim), positions
    ).astype(jnp.bfloat16)
    offset = my_index * local_count
    near = lax.dynamic_slice_in_dim(window, offset, reach + local_count, 0)
    key_global = window_start + offset + jnp.arange(reach + local_count, dtype=jnp.int32)
    query_global = jnp.repeat(
        group_index * span + offset + jnp.arange(local_count, dtype=jnp.int32), GROUP
    )
    query_places = jnp.repeat(positions, GROUP)
    results = attend_rows(
        rotated.reshape(local_count * GROUP, head_dim),
        query_global,
        query_places,
        near[:, :head_dim],
        near[:, head_dim:],
        key_global,
    )
    attention = results.reshape(local_count, GROUP * head_dim)
    return (attention, new_master, new_first, new_second)


def rope_tables(places, width):
    lane = lax.broadcasted_iota(jnp.int32, (1, width), 1)
    half_width = width // 2
    slot = jnp.where(lane < half_width, lane, lane - half_width).astype(jnp.float32)
    freqs = jnp.exp(slot * (-2.0 * math.log(rope_base) / width))
    angles = places.astype(jnp.float32) * freqs
    sine = jnp.sin(angles)
    return jnp.cos(angles), jnp.where(lane < half_width, -sine, sine)


def fused_kernel(
    tok_hbm, query_hbm, weight_ref, places_hbm, out_ref,
    places_ref, own_scores, probs, tok, blocks, query, rotated, part, back, past_keys, past_values, places, cosine, sine,
    tok_sem, tok_send, tok_recv, query_sem, places_sem, weight_sem, piece_recv,
    x_send, y_send, z_send, cross_send, half_x_send, half_y_send, across_send,
    back_sems, kv_send, kv_recv,
):
    z = lax.axis_index("dp")
    seq = lax.axis_index("seq")
    planes = lax.axis_size("dp")
    wide = lax.axis_size("seq")
    core = lax.rem(seq, 2)
    x = lax.rem(seq // 2, 2)
    y = seq // 4
    count = tok_hbm.shape[0]
    depth = weight_ref.shape[0]
    half = depth // 2
    head_dim = weight_ref.shape[1] // 2
    me = z * wide + seq
    total = planes * wide
    chips = blocks.shape[0]

    def ordinal(index):
        return (index // wide, lax.rem(index, wide))

    peer = (z, seq + 1 - 2 * core)
    x_side = (z, seq + 2 - 4 * x)
    y_side = (z, seq + 4 - 8 * y)
    z_pair = z + 1 - 2 * lax.rem(z, 2)
    pair_side = (z_pair, seq)
    cross_side = (3 - z, seq)
    inner = (z == 1) | (z == 2)
    next_one, next_two = lax.rem(me + 1, total), lax.rem(me + 2, total)
    last_one, last_two = lax.rem(me + total - 1, total), lax.rem(me + total - 2, total)

    barrier = pltpu.get_barrier_semaphore()
    greeted = [peer, x_side, y_side, pair_side, cross_side]
    greeted += [ordinal(index) for index in (next_one, next_two, last_one, last_two)]
    for device in greeted:
        pl.semaphore_signal(barrier, inc=1, device_id=device, device_id_type=MESH)

    def columns(chip, which):
        return pl.ds(pl.multiple_of((chip * 2 + which) * depth, depth), depth)

    def rows_of(which):
        return pl.ds(pl.multiple_of(which * count, count), count)

    def local_tokens(chip):
        return pltpu.make_async_copy(
            tok_hbm.at[:, columns(chip, core)], tok.at[chip, rows_of(core)], tok_sem.at[chip]
        )

    def sent_tokens(chip):
        return pltpu.make_async_remote_copy(
            src_ref=tok_hbm.at[:, columns(chip, 1 - core)],
            dst_ref=tok.at[chip, rows_of(core)],
            send_sem=tok_send.at[chip],
            recv_sem=tok_recv.at[chip],
            device_id=peer,
            device_id_type=MESH,
        )

    query_copy = pltpu.make_async_copy(query_hbm, query, query_sem)
    places_copy = pltpu.make_async_copy(places_hbm, places_ref, places_sem)
    query_copy.start()
    places_copy.start()
    pl.semaphore_wait(barrier, len(greeted))

    order = [z, z_pair, 2 - z // 2, 3 - 3 * (z // 2)]

    def chip_at(plane, y_at, x_at):
        return plane * 4 + y_at * 2 + x_at

    spots = {"line": (y, x), "along_x": (y, 1 - x), "along_y": (1 - y, x), "corner": (1 - y, 1 - x)}

    def chip_of(kind, step):
        return chip_at(order[step], *spots[kind])

    def send_piece(kind, step, which, device, sem):
        chip = chip_of(kind, step)
        rows = pl.ds(which * half, half)
        own_block = kind == "line" and step == 0
        return pltpu.make_async_remote_copy(
            src_ref=weight_ref.at[rows] if own_block else blocks.at[chip, rows],
            dst_ref=blocks.at[chip, rows],
            send_sem=sem,
            recv_sem=piece_recv.at[which, chip],
            device_id=device,
            device_id_type=MESH,
        )

    def send_line(step, which, side):
        device, sem = {
            "x": (x_side, x_send),
            "y": (y_side, y_send),
            "pair": (pair_side, z_send),
            "cross": (cross_side, cross_send),
        }[side]
        return send_piece("line", step, which, device, sem.at[2 * step + which])

    def send_half(step, which):
        if which == 0:
            return send_piece("along_x", step, 0, y_side, half_y_send.at[step])
        return send_piece("along_y", step, 1, x_side, half_x_send.at[step])

    def send_corner(which, side):
        device, offset = {"pair": (pair_side, 0), "cross": (cross_side, 2)}[side]
        return send_piece("corner", 0, which, device, across_send.at[offset + which])

    arrived = set()

    def arrive(kind, step, which):
        if (kind, step, which) not in arrived:
            arrived.add((kind, step, which))
            chip = chip_of(kind, step)
            place = blocks.at[chip, pl.ds(which * half, half)]
            pltpu.make_async_copy(place, place, piece_recv.at[which, chip]).wait()

    def add_block(chip, source):
        local_tokens(chip).wait()
        sent_tokens(chip).wait_recv()
        part[...] += jnp.dot(tok[chip], source[...], preferred_element_type=jnp.float32)

    def add(kind, step):
        arrive(kind, step, 0)
        arrive(kind, step, 1)
        chip = chip_of(kind, step)
        add_block(chip, blocks.at[chip])

    steps = len(order)
    for which in range(2):
        for side in ("x", "y", "pair"):
            send_line(0, which, side).start()

        @pl.when(inner)
        def _():
            send_line(0, which, "cross").start()

    own_place = blocks.at[chip_of("line", 0)]
    weight_copy = pltpu.make_async_copy(weight_ref, own_place, weight_sem)
    weight_copy.start()

    @pl.loop(0, chips)
    def _(chip):
        sent_tokens(chip).start()
        local_tokens(chip).start()

    part[...] = jnp.zeros_like(part)

    def rotate(values_in):
        return values_in * cosine[...] + pltpu.roll(values_in, head_dim // 2, 1) * sine[...]

    def forward_half(step, which):
        arrive("along_y" if which else "along_x", step, which)
        send_half(step, which).start()

    def forward_line(step, which, onward=None):
        arrive("line", step, which)
        if onward is not None:
            send_line(step, which, onward).start()
        send_line(step, which, "x").start()
        send_line(step, which, "y").start()

    row = lax.broadcasted_iota(jnp.int32, (count, count), 0)
    lane = lax.broadcasted_iota(jnp.int32, (count, count), 1)
    heads = query.shape[1] // head_dim

    def prepare():
        places_copy.wait()
        places[...] = jnp.sum(
            jnp.where(row == lane, places_ref[...].astype(jnp.float32), 0.0),
            axis=1,
            keepdims=True,
        )
        cosine[...], sine[...] = rope_tables(places[...], head_dim)
        query_copy.wait()
        for head in range(heads):
            at = slice(head * head_dim, (head + 1) * head_dim)
            rotated[:, at] = rotate(query[:, at].astype(jnp.float32)).astype(jnp.bfloat16)

    outer = (z == 0) | (z == 3)

    @pl.when(inner)
    def _():
        arrived.clear()
        for which in range(2):
            forward_half(0, which)
            forward_line(1, which, "cross")
            forward_line(2, which, "pair")
        weight_copy.wait()
        add_block(chip_of("line", 0), own_place)
        for which in range(2):
            arrive("corner", 0, which)
            send_corner(which, "cross").start()
        for which in range(2):
            forward_line(3, which, "pair")
        for which in range(2):
            send_corner(which, "pair").start()
        for item in (("along_x", 0), ("along_y", 0), ("line", 1), ("line", 2), ("corner", 0)):
            add(*item)
        prepare()
        for item in (("along_x", 1), ("along_y", 1), ("along_x", 2), ("along_y", 2)):
            add(*item)
        forward_half(3, 0)
        forward_half(3, 1)
        for item in (("line", 3), ("corner", 1), ("along_x", 3), ("along_y", 3)):
            add(*item)
        add("corner", 2)
        add("corner", 3)

    @pl.when(outer)
    def _():
        arrived.clear()
        for which in range(2):
            forward_half(0, which)
            forward_line(1, which)
        weight_copy.wait()
        add_block(chip_of("line", 0), own_place)
        for which in range(2):
            arrive("corner", 0, which)
            send_corner(which, "pair").start()
        forward_line(2, 0)
        forward_line(2, 1)
        for item in (("along_x", 0), ("along_y", 0), ("line", 1), ("corner", 0)):
            add(*item)
        forward_line(3, 0)
        forward_line(3, 1)
        prepare()
        for item in (("along_x", 1), ("along_y", 1), ("line", 2)):
            add(*item)
        forward_half(2, 0)
        forward_half(2, 1)
        add("along_x", 2)
        add("along_y", 2)
        forward_half(3, 0)
        forward_half(3, 1)
        for item in (("line", 3), ("corner", 1), ("along_x", 3), ("along_y", 3)):
            add(*item)
        add("corner", 2)
        add("corner", 3)

    sides = (pl.ds(0, head_dim), pl.ds(head_dim, head_dim))

    def back_copy(side):
        return pltpu.make_async_remote_copy(
            src_ref=part.at[rows_of(1 - core), sides[side]],
            dst_ref=back.at[:, sides[side]],
            send_sem=back_sems.at[0, side],
            recv_sem=back_sems.at[1, side],
            device_id=peer,
            device_id_type=MESH,
        )

    own = pl.ds(2 * count, count)
    pasts = (past_keys, past_values)

    def send_past(side, distance):
        return pltpu.make_async_remote_copy(
            src_ref=pasts[side].at[own],
            dst_ref=pasts[side].at[pl.ds((2 - distance) * count, count)],
            send_sem=kv_send.at[side, distance - 1],
            recv_sem=kv_recv.at[side, distance - 1],
            device_id=ordinal(next_one if distance == 1 else next_two),
            device_id_type=MESH,
        )

    back_copy(0).start()
    back_copy(1).start()
    for side in range(2):
        back_copy(side).wait_recv()
        projected = part[rows_of(core), sides[side]] + back[:, sides[side]]
        if side == 0:
            projected = rotate(projected)
        pasts[side][own, :] = projected.astype(jnp.bfloat16)
        for distance in (2, 1):

            @pl.when(me < total - distance)
            def _():
                send_past(side, distance).start()

            @pl.when(me < distance)
            def _():
                pasts[side][pl.ds((2 - distance) * count, count), :] = jnp.zeros(
                    (count, head_dim), jnp.bfloat16
                )

    def past_arrival(side):
        for distance in (1, 2):

            @pl.when(me >= distance)
            def _():
                send_past(side, distance).wait_recv()

    near_limit = row - places[...].astype(jnp.int32)
    early = lax.broadcasted_iota(jnp.int32, (count, 2 * count), 1) - 2 * count
    allowed_own = (lane <= row) & (lane >= near_limit)
    allowed_early = early >= near_limit[:, :1]

    def score(head, keys, allowed):
        scores = lax.dot_general(
            rotated[:, head * head_dim : (head + 1) * head_dim],
            keys,
            (((1,), (1,)), ((), ())),
            preferred_element_type=jnp.float32,
        ) * head_dim ** (-0.5)
        return jnp.where(allowed, scores, masked_score)

    own_keys = past_keys[own, :]
    for head in range(heads):
        own_scores[head] = score(head, own_keys, allowed_own)

    past = pl.ds(0, 2 * count)
    past_arrival(0)
    early_keys = past_keys[past, :]
    for head in range(heads):
        near = own_scores[head]
        far = score(head, early_keys, allowed_early)
        top = jnp.maximum(
            jnp.max(near, axis=1, keepdims=True), jnp.max(far, axis=1, keepdims=True)
        )
        near = jnp.exp(near - top)
        far = jnp.exp(far - top)
        share = 1.0 / (
            jnp.sum(near, axis=1, keepdims=True) + jnp.sum(far, axis=1, keepdims=True)
        )
        probs[head, :, : 2 * count] = (far * share).astype(jnp.bfloat16)
        probs[head, :, 2 * count :] = (near * share).astype(jnp.bfloat16)
    past_arrival(1)
    values_v = past_values[...]
    for head in range(heads):
        out_ref[:, head * head_dim : (head + 1) * head_dim] = jnp.dot(
            probs[head], values_v, preferred_element_type=jnp.float32
        ).astype(jnp.bfloat16)

    for which in range(2):
        for step in range(steps):
            send_line(step, which, "x").wait_send()
            send_line(step, which, "y").wait_send()
        send_half(0, which).wait_send()
        send_half(3, which).wait_send()
        send_line(0, which, "pair").wait_send()
        send_corner(which, "pair").wait_send()

        @pl.when(outer)
        def _():
            send_half(2, which).wait_send()

        @pl.when(inner)
        def _():
            send_line(2, which, "pair").wait_send()
            send_line(3, which, "pair").wait_send()
            send_line(0, which, "cross").wait_send()
            send_line(1, which, "cross").wait_send()
            send_corner(which, "cross").wait_send()

    @pl.loop(0, chips)
    def _(chip):
        sent_tokens(chip).wait_send()

    for side in range(2):
        back_copy(side).wait_send()
        for distance in (1, 2):

            @pl.when(me < total - distance)
            def _():
                send_past(side, distance).wait_send()


def fused_local(tokens, queries, positions, grad, master, moment1, moment2, step):
    new_master, new_first, new_second = adam_update(grad, master, moment1, moment2, step)
    weight = new_master.astype(jnp.bfloat16)
    count = tokens.shape[0]
    depth, width = weight.shape
    head_dim = width // 2
    chips = tokens.shape[1] // depth // 2
    dma = pltpu.SemaphoreType.DMA
    anywhere = pl.BlockSpec(memory_space=pl.ANY)
    inside = pl.BlockSpec(memory_space=pltpu.VMEM)
    attention = pl.pallas_call(
        fused_kernel,
        out_shape=pltpu.VMEM(queries.shape, jnp.bfloat16),
        in_specs=[anywhere, anywhere, anywhere, anywhere],
        out_specs=inside,
        scratch_shapes=[
            pltpu.VMEM((1, count), jnp.int32),
            pltpu.VMEM((queries.shape[1] // head_dim, count, count), jnp.float32),
            pltpu.VMEM((queries.shape[1] // head_dim, count, 3 * count), jnp.bfloat16),
            pltpu.VMEM((chips, 2 * count, depth), jnp.bfloat16),
            pltpu.VMEM((chips, depth, width), jnp.bfloat16),
            pltpu.VMEM(queries.shape, jnp.bfloat16),
            pltpu.VMEM(queries.shape, jnp.bfloat16),
            pltpu.VMEM((2 * count, width), jnp.float32),
            pltpu.VMEM((count, width), jnp.float32),
            pltpu.VMEM((3 * count, head_dim), jnp.bfloat16),
            pltpu.VMEM((3 * count, head_dim), jnp.bfloat16),
            pltpu.VMEM((count, 1), jnp.float32),
            pltpu.VMEM((count, head_dim), jnp.float32),
            pltpu.VMEM((count, head_dim), jnp.float32),
            dma((chips,)), dma((chips,)), dma((chips,)), dma, dma, dma,
            dma((2, chips)),
            dma((8,)), dma((8,)), dma((8,)), dma((4,)), dma((4,)), dma((4,)), dma((4,)),
            dma((2, 2)), dma((2, 2)), dma((2, 2)),
        ],
        compiler_params=pltpu.CompilerParams(
            collective_id=0, has_side_effects=True, vmem_limit_bytes=121 * 512 * 1024
        ),
    )(tokens, queries, weight, positions.reshape(1, -1))
    return (attention, new_master, new_first, new_second)


def solution(mesh):
    small = (mesh.shape["dp"], mesh.shape["seq"]) == (4, 8)
    return jax.shard_map(
        fused_local if small else local,
        mesh=mesh,
        in_specs=(
            P(("dp", "seq"), None),
            P(("dp", "seq"), None),
            P(("dp", "seq")),
            P(("dp", "seq"), None),
            P(("dp", "seq"), None),
            P(("dp", "seq"), None),
            P(("dp", "seq"), None),
            P(),
        ),
        out_specs=(
            P(("dp", "seq"), None),
            P(("dp", "seq"), None),
            P(("dp", "seq"), None),
            P(("dp", "seq"), None),
        ),
        check_vma=False,
    )
```
